512 devices in a mesh: pp: 16 (over z, core), ep: 32 (over x, y).
Axes of the slice: x: 4, y: 8, z: 8, core: 2. Of those that a mesh axis runs over, the one named last changes fastest.
Arguments:
- tokens: bfloat16 [16, 4096, 3584], P('pp', 'ep'), may hold values from -6 to 6
- cotangent: bfloat16 [16, 4096, 3584], P('pp', 'ep'), may hold values from -6 to 6
- expert_slot: int32 [16, 4096], P('pp', 'ep'), may hold values from 0 to 2, as said below
- gate_fixed: int32 [16, 4096], P('pp', 'ep'), may hold values from 256 to 4095
- w_gate: bfloat16 [16, 2048, 3584], P('pp', 'ep')
- w_up: bfloat16 [16, 2048, 3584], P('pp', 'ep')
- w_down: bfloat16 [16, 2048, 3584], P('pp', 'ep')
Outputs:
- input_grad: bfloat16 [16, 4096, 3584], P('pp', 'ep')
- grad_gate: bfloat16 [16, 2048, 1792], P('pp', 'ep')
- grad_up: bfloat16 [16, 2048, 1792], P('pp', 'ep')
- grad_down: bfloat16 [16, 2048, 1792], P('pp', 'ep')
The draws below stay inside these ranges and needn't reach their ends.
Inputs may be any that keep to these rules, and one draw needn't show every extreme that they name: `expert_slot`: 2 means the token uses none of the window's experts. In every block of 128 consecutive tokens of one device at most 16 tokens name one expert, and in each copy's microbatch one expert is named by exactly 16 tokens of every block. `gate_fixed`: the gate weight is this value divided by 4096.
All inputs are finite; a program needn't handle non-finite values.
Results may differ from the reference program's by a relative error of at most 0.0065.
Values may be sent and summed in bfloat16 or wider, within the bound.
No kernel may reach another device: no remote copies, remote signals or barrier semaphores. Data moves between devices by JAX's collectives and lax.ppermute only.
A program may use at most 128 MiB of HBM per device.

```python
import math
import jax
import jax.numpy as jnp
from jax import lax

D = 3584
H_DEV = 64
E_WIN = 2
T_DEV = 128
COPIES = 16
HID = 1024
HID_ALL = 2048
TOKENS = 4096
CAP = 16
N_EP = 32


def mirrored(key, scale):
    half_copy = jax.random.normal(key, (COPIES // 2, HID_ALL, D), jnp.float32) * scale
    return jnp.concatenate([half_copy, half_copy[::-1]], axis=0)


def draw_w_gate(key, part):
    key = jax.random.fold_in(key, 11)
    return mirrored(key, 1.0 / math.sqrt(D)).astype(jnp.bfloat16)


def draw_w_up(key, part):
    key = jax.random.fold_in(key, 12)
    return mirrored(key, 1.0 / math.sqrt(D)).astype(jnp.bfloat16)


def draw_w_down(key, part):
    key = jax.random.fold_in(key, 13)
    return mirrored(key, 1.0 / math.sqrt(HID)).astype(jnp.bfloat16)


def block_ranks(order_key):
    return jnp.argsort(jax.random.permutation(order_key, T_DEV)).astype(jnp.int32)


def draw_expert_slot(key, part):
    key = jax.random.fold_in(key, 5)
    blocks_per_copy = TOKENS // T_DEV
    block_count = COPIES * blocks_per_copy
    key_hot, key_count, key_order = jax.random.split(key, 3)
    hottest = jax.random.randint(key_hot, (COPIES, 1), 0, E_WIN)
    hottest = jnp.repeat(hottest, blocks_per_copy, axis=0)
    counts = jax.random.randint(key_count, (block_count, E_WIN), CAP // 4, CAP + 1)
    counts = jnp.where(jnp.arange(E_WIN)[None, :] == hottest, CAP, counts)
    bounds = jnp.cumsum(counts, axis=1)
    ranks = jax.vmap(block_ranks)(jax.random.split(key_order, block_count))
    slot_ids = jnp.sum((ranks[:, :, None] >= bounds[:, None, :]).astype(jnp.int32), axis=2)
    return slot_ids.reshape(COPIES, TOKENS).astype(jnp.int32)


def plant(array, rng, least, top_value):
    dims = array.shape
    index_at = [jax.random.randint(jax.random.fold_in(rng, axis), (), 0, dims[axis]) for axis in range(len(dims))]
    array = array.at[tuple(index_at)].set(least)
    longest = dims.index(max(dims))
    index_at[longest] = (index_at[longest] + 1) % dims[longest]
    return array.at[tuple(index_at)].set(top_value)


def block_scale(key, dims, cuts, low, high):
    factor_of, own = 1.0, jax.random.fold_in(key, 6)
    for axis_at, blocks in cuts:
        steps = jnp.exp(jax.random.uniform(jax.random.fold_in(own, axis_at), (blocks,), jnp.float32, low / len(cuts), high / len(cuts)))
        factor_of = factor_of * jnp.repeat(steps, dims[axis_at] // blocks).reshape([-1 if axis == axis_at else 1 for axis in range(len(dims))])
    return factor_of


def bell_draw(stream_key, shape, scale, bound, cuts=(), held_as=jnp.bfloat16):
    drawn = scale * jax.random.normal(stream_key, shape, jnp.float32)
    if cuts:
        drawn = drawn * block_scale(stream_key, shape, cuts, -0.22, 0.18)
    return jnp.clip(drawn, -bound, bound).astype(held_as)


def setup_inputs(seed: int = 0) -> dict:
    streams_of = jax.random.split(jax.random.key(seed), 8)
    return {
        "tokens": bell_draw(streams_of[0], (COPIES, TOKENS, D), 1.0, 6.0, ((0, 16), (1, 32))),
        "cotangent": bell_draw(streams_of[1], (COPIES, TOKENS, D), 1.0, 6.0, ((0, 16), (1, 32))),
        "expert_slot": draw_expert_slot(jax.random.fold_in(streams_of[7], 71), 0),
        "gate_fixed": plant(jax.random.randint(streams_of[3], (COPIES, TOKENS), 256, 4096), jax.random.fold_in(streams_of[3], 1), 256, 4095).astype(jnp.int32),
        "w_gate": draw_w_gate(jax.random.fold_in(streams_of[7], 71), 0),
        "w_up": draw_w_up(jax.random.fold_in(streams_of[7], 71), 0),
        "w_down": draw_w_down(jax.random.fold_in(streams_of[7], 71), 0),
    }


def slot_numbers(block_ids):
    onehot = (block_ids[:, None] == jnp.arange(E_WIN, dtype=jnp.int32)[None, :]).astype(jnp.int32)
    rank_in = lax.optimization_barrier(jnp.sum(jnp.cumsum(onehot, axis=0) * onehot, axis=1)) - 1
    return jnp.where(block_ids < E_WIN, block_ids * CAP + rank_in, -1)

def selector(block_ids):
    slot_rows = slot_numbers(block_ids)
    return slot_rows[None, :] == jnp.arange(E_WIN * CAP, dtype=jnp.int32)[:, None]

def silu_grad(pre_value):
    sigmoid_value = jax.nn.sigmoid(pre_value)
    return sigmoid_value * (1.0 + pre_value * (1.0 - sigmoid_value))

def one_copy(inputs):
    tokens_c, cot_c, slot_ids, gate_ints, weight_g, weight_u, weight_d = inputs
    members = N_EP // E_WIN
    gate_value = gate_ints.astype(jnp.float32) / 4096.0
    scaled = (gate_value[:, None] * cot_c.astype(jnp.float32)).astype(jnp.bfloat16)
    select = jax.vmap(selector)(slot_ids.reshape(N_EP, T_DEV)).astype(jnp.float32)
    packed_x = jnp.einsum('bst,btd->bsd', select, tokens_c.reshape(N_EP, T_DEV, D).astype(jnp.float32)).astype(jnp.bfloat16)
    packed_c = jnp.einsum('bst,btd->bsd', select, scaled.reshape(N_EP, T_DEV, D).astype(jnp.float32)).astype(jnp.bfloat16)
    packed_x = packed_x.reshape(N_EP, E_WIN, CAP, D).transpose(1, 0, 2, 3).reshape(E_WIN, N_EP * CAP, D)
    packed_c = packed_c.reshape(N_EP, E_WIN, CAP, D).transpose(1, 0, 2, 3).reshape(E_WIN, N_EP * CAP, D)
    expert_g = weight_g.reshape(E_WIN, HID, D)
    expert_u = weight_u.reshape(E_WIN, HID, D)
    expert_d = weight_d.reshape(E_WIN, HID, D)
    contract_rows = (((1,), (1,)), ((), ()))
    contract_first = (((0,), (0,)), ((), ()))
    grads_g = []
    grads_u = []
    grads_d = []
    contribs = []
    for expert in range(E_WIN):
        rows_x = packed_x[expert]
        rows_c = packed_c[expert]
        gate_pre = lax.dot_general(rows_x, expert_g[expert], contract_rows, preferred_element_type=jnp.float32)
        up_pre = lax.dot_general(rows_x, expert_u[expert], contract_rows, preferred_element_type=jnp.float32)
        activated = jax.nn.silu(gate_pre)
        hidden = (activated * up_pre).astype(jnp.bfloat16)
        hidden_cot = lax.dot_general(rows_c, expert_d[expert], contract_rows, preferred_element_type=jnp.float32)
        gate_cot = (hidden_cot * up_pre * silu_grad(gate_pre)).astype(jnp.bfloat16)
        up_cot = (hidden_cot * activated).astype(jnp.bfloat16)
        grads_d.append(lax.dot_general(hidden, rows_c, contract_first, preferred_element_type=jnp.float32).astype(jnp.bfloat16))
        grads_g.append(lax.dot_general(gate_cot, rows_x, contract_first, preferred_element_type=jnp.float32).astype(jnp.bfloat16))
        grads_u.append(lax.dot_general(up_cot, rows_x, contract_first, preferred_element_type=jnp.float32).astype(jnp.bfloat16))
        row_count = N_EP * CAP
        pieces = jnp.einsum('rkh,khd->krd', gate_cot.reshape(row_count, members, H_DEV).astype(jnp.float32), expert_g[expert].reshape(members, H_DEV, D).astype(jnp.float32))
        pieces = pieces + jnp.einsum('rkh,khd->krd', up_cot.reshape(row_count, members, H_DEV).astype(jnp.float32), expert_u[expert].reshape(members, H_DEV, D).astype(jnp.float32))
        contribs.append(lax.optimization_barrier(jnp.sum(pieces.astype(jnp.bfloat16).astype(jnp.float32), axis=0)))
    contrib = jnp.stack(contribs).reshape(E_WIN, N_EP, CAP, D).transpose(1, 0, 2, 3).reshape(N_EP, E_WIN * CAP, D)
    branch = jnp.einsum('bst,bsd->btd', select, contrib, precision=lax.Precision.HIGHEST)
    input_grad = (cot_c.astype(jnp.float32) + branch.reshape(TOKENS, D)).astype(jnp.bfloat16)
    return (input_grad, jnp.concatenate(grads_g, axis=0), jnp.concatenate(grads_u, axis=0), jnp.concatenate(grads_d, axis=0))

def reference(tokens, cotangent, expert_slot, gate_fixed, w_gate, w_up, w_down):
    input_grad, copy_g, copy_u, copy_d = lax.map(one_copy, (tokens, cotangent, expert_slot, gate_fixed, w_gate, w_up, w_down))
    half_width = D // 2
    upper_side = (jnp.arange(COPIES) >= COPIES // 2)[:, None, None]

    def pair_sum(copy_grads):
        pair_total = (copy_grads.astype(jnp.float32) + copy_grads[::-1].astype(jnp.float32)).astype(jnp.bfloat16)
        return jnp.where(upper_side, pair_total[:, :, half_width:], pair_total[:, :, :half_width])
    return (input_grad, pair_sum(copy_g), pair_sum(copy_u), pair_sum(copy_d))
```

```python
import jax
import jax.numpy as jnp
from jax import lax
from jax.sharding import PartitionSpec as P

E_WIN = 2
CAP = 16
NX = 4
NY = 8
BF = jnp.bfloat16
F32 = jnp.float32


def swap_x_outer(v):
    return lax.ppermute(v, "ep", [(i, (NX - 1 - i // NY) * NY + i % NY) for i in range(NX * NY)])


def swap_x_pair(v):
    return lax.ppermute(v, "ep", [(i, i ^ NY) for i in range(NX * NY)])


def shift_y(v, step):
    return lax.ppermute(
        v, "ep", [(i, i // NY * NY + (i + step) % NY) for i in range(NX * NY)]
    )


def mirror(v):
    n = lax.axis_size("pp")
    return lax.ppermute(v, "pp", [(i, n - 1 - i) for i in range(n)])


def row_selector(block_ids, own_expert):
    onehot = (block_ids[:, None] == jnp.arange(E_WIN, dtype=jnp.int32)[None, :]).astype(jnp.int32)
    rank_in = jnp.sum(jnp.cumsum(onehot, axis=0) * onehot, axis=1) - 1
    relative = block_ids ^ own_expert
    slot = jnp.where(block_ids < E_WIN, relative * CAP + rank_in, -1)
    return slot[None, :] == jnp.arange(E_WIN * CAP, dtype=jnp.int32)[:, None]


def dot(a, b, dims):
    return lax.dot_general(a, b, (dims, ((), ())), preferred_element_type=F32)


def shards(tokens, cotangent, expert_slot, gate_fixed, w_gate, w_up, w_down):
    block_x, block_cot = tokens[0], cotangent[0]
    width = block_x.shape[1]
    half = width // 2
    h_dev = w_gate.shape[1]
    own_expert = lax.axis_index("ep") // (NX * NY // E_WIN)
    upper = lax.axis_index("pp") >= lax.axis_size("pp") // 2

    select = row_selector(expert_slot[0], own_expert).astype(BF)
    gate_value = gate_fixed[0].astype(F32) / 4096.0
    scaled = (gate_value[:, None] * block_cot.astype(F32)).astype(BF)
    packed_x = dot(select, block_x, ((1,), (0,))).astype(BF)
    packed_c = dot(select, scaled, ((1,), (0,))).astype(BF)
    other = swap_x_outer(jnp.concatenate([packed_x[CAP:], packed_c[CAP:]], axis=0))
    chunk = jnp.concatenate([packed_x[:CAP], other[:CAP], packed_c[:CAP], other[CAP:]], axis=0)
    rows = 2 * CAP

    mine = jnp.concatenate([w_gate[0], w_up[0], w_down[0]], axis=0)
    theirs = swap_x_pair(mine)

    right = left = chunk
    lefts, rights = [], []
    for step in range(3):
        right = shift_y(right, 1)
        left = shift_y(left, -1)
        rights.append(right)
        lefts.append(left)
    far_x = shift_y(right[:rows], 1)
    far_c = shift_y(left[rows:], -1)
    near = [chunk]
    for r, l in zip(rights, lefts):
        near += [r, l]
    rows_x = jnp.concatenate([p[:rows] for p in near] + [far_x], axis=0)
    rows_c = jnp.concatenate([p[rows:] for p in near] + [far_c], axis=0)

    h = h_dev
    w_gu = jnp.concatenate([mine[: 2 * h], theirs[: 2 * h]], axis=0)
    w_d = jnp.concatenate([mine[2 * h :], theirs[2 * h :]], axis=0)
    pre = dot(rows_x, w_gu, ((1,), (1,)))
    gate_pre = jnp.concatenate([pre[:, :h], pre[:, 2 * h : 3 * h]], axis=1)
    up_pre = jnp.concatenate([pre[:, h : 2 * h], pre[:, 3 * h :]], axis=1)
    sig = jax.nn.sigmoid(gate_pre)
    activated = gate_pre * sig
    hidden = (activated * up_pre).astype(BF)
    hidden_cot = dot(rows_c, w_d, ((1,), (1,)))
    gate_cot = (hidden_cot * up_pre * (sig * (1.0 + gate_pre * (1.0 - sig)))).astype(BF)
    up_cot = (hidden_cot * activated).astype(BF)
    gu_cot = jnp.concatenate([gate_cot[:, :h], up_cot[:, :h], gate_cot[:, h:], up_cot[:, h:]], axis=1)
    partial = dot(gu_cot, w_gu, ((1,), (0,))).astype(BF).reshape(NY, rows, width)

    def plus(a, b):
        return (a.astype(F32) + b.astype(F32)).astype(BF)

    go_right = shift_y(partial[7][:CAP], 1)
    go_left = shift_y(partial[7][CAP:], -1)
    go_right = jnp.concatenate([plus(partial[6][:CAP], go_right), partial[6][CAP:]], axis=0)
    go_left = jnp.concatenate([partial[5][:CAP], plus(partial[5][CAP:], go_left)], axis=0)
    go_right, go_left = shift_y(go_right, 1), shift_y(go_left, -1)
    go_right, go_left = shift_y(plus(partial[4], go_right), 1), shift_y(plus(partial[3], go_left), -1)
    go_right, go_left = shift_y(plus(partial[2], go_right), 1), shift_y(plus(partial[1], go_left), -1)
    summed = (partial[0].astype(F32) + go_right.astype(F32) + go_left.astype(F32)).astype(BF)
    back = swap_x_outer(summed[CAP:])
    branch = dot(select, jnp.concatenate([summed[:CAP], back], axis=0), ((0,), (0,)))
    input_grad = (block_cot.astype(F32) + branch).astype(BF)[None]

    grad_gu = dot(gu_cot, rows_x, ((0,), (0,)))
    grad_d = dot(hidden, rows_c, ((0,), (0,)))
    grad_own = jnp.concatenate([grad_gu[: 2 * h], grad_d[:h]], axis=0).astype(BF)
    grad_their = jnp.concatenate([grad_gu[2 * h :], grad_d[h:]], axis=0).astype(BF)

    def keep_send(v):
        low, high = v[:, :half], v[:, half:]
        return jnp.where(upper, high, low), jnp.where(upper, low, high)

    keep_own, send_own = keep_send(grad_own)
    keep_their, send_their = keep_send(grad_their)
    got_send = swap_x_pair(send_their)
    got_keep = swap_x_pair(keep_their)
    got = mirror(plus(send_own, got_send))
    total = (keep_own.astype(F32) + got_keep.astype(F32) + got.astype(F32)).astype(BF)
    return (input_grad, total[None, :h], total[None, h : 2 * h], total[None, 2 * h :])


def solution(mesh):
    wide = P("pp", "ep", None)
    flat = P("pp", "ep")
    return jax.shard_map(
        shards,
        mesh=mesh,
        in_specs=(wide, wide, flat, flat, wide, wide, wide),
        out_specs=(wide, wide, wide, wide),
        check_vma=False,
    )
```

```python
import jax
import jax.numpy as jnp
from jax import lax
from jax.experimental import pallas as pl
from jax.experimental.pallas import tpu as pltpu
from jax.sharding import PartitionSpec as P

E_WIN = 2
CAP = 16
NX = 4
NY = 8
BF = jnp.bfloat16
F32 = jnp.float32


def swap_x_outer(v):
    return lax.ppermute(v, "ep", [(i, (NX - 1 - i // NY) * NY + i % NY) for i in range(NX * NY)])


def swap_x_pair(v):
    return lax.ppermute(v, "ep", [(i, i ^ NY) for i in range(NX * NY)])


def shift_y(v, step):
    return lax.ppermute(
        v, "ep", [(i, i // NY * NY + (i + step) % NY) for i in range(NX * NY)]
    )


def mirror(v):
    n = lax.axis_size("pp")
    return lax.ppermute(v, "pp", [(i, n - 1 - i) for i in range(n)])


def dot(a, b, dims):
    return lax.dot_general(a, b, (dims, ((), ())), preferred_element_type=F32)


def plus(a, b):
    return (a.astype(F32) + b.astype(F32)).astype(BF)


def after(v, *others):
    return lax.optimization_barrier((v, *others))[0]


def pack_kernel(
    expert_ref, slot_hbm, gate_hbm, x_hbm, c_hbm, own_ref, other_ref, select_ref,
    slot_ref, gate_ref, x_ref, c_ref, sems,
):
    pairs = ((slot_hbm, slot_ref), (gate_hbm, gate_ref), (x_hbm, x_ref), (c_hbm, c_ref))
    copies = [pltpu.make_async_copy(src, dst, sems.at[i]) for i, (src, dst) in enumerate(pairs)]
    for copy in copies:
        copy.start()
    copies[0].wait()
    copies[1].wait()
    slots = slot_ref[...]
    n = slots.shape[1]
    expert = expert_ref[0]
    earlier = lax.broadcasted_iota(jnp.int32, (n, n), 0) < lax.broadcasted_iota(jnp.int32, (n, n), 1)
    earlier = jnp.where(earlier, 1.0, 0.0).astype(BF)
    want = lax.broadcasted_iota(jnp.int32, (CAP, n), 0).astype(F32)

    def pick(which):
        named = jnp.where(slots == which, 1.0, 0.0)
        named = jnp.broadcast_to(named, (CAP, n))
        rank = jnp.dot(named.astype(BF), earlier, preferred_element_type=F32)
        return jnp.where(rank == want, named, 0.0)

    select = jnp.concatenate([pick(expert), pick(1 - expert)], axis=0)
    gate = jnp.sum(select * (gate_ref[...].astype(F32) / 4096.0), axis=1, keepdims=True)
    select = select.astype(BF)
    select_ref[...] = select
    copies[2].wait()
    picked = jnp.dot(select, x_ref[...], preferred_element_type=F32).astype(BF)
    own_ref[:CAP] = picked[:CAP]
    other_ref[:CAP] = picked[CAP:]
    copies[3].wait()
    picked = (gate * jnp.dot(select, c_ref[...], preferred_element_type=F32)).astype(BF)
    own_ref[CAP:] = picked[:CAP]
    other_ref[CAP:] = picked[CAP:]


def pack(expert, slots, gates, block_x, block_cot):
    width = block_x.shape[1]
    vmem = pl.BlockSpec(memory_space=pltpu.VMEM)
    hbm = pl.BlockSpec(memory_space=pltpu.HBM)
    operands = (slots, gates, block_x, block_cot)
    return pl.pallas_call(
        pack_kernel,
        out_shape=(
            jax.ShapeDtypeStruct((2 * CAP, width), BF),
            jax.ShapeDtypeStruct((2 * CAP, width), BF),
            jax.ShapeDtypeStruct((E_WIN * CAP, block_x.shape[0]), BF),
        ),
        in_specs=[pl.BlockSpec(memory_space=pltpu.SMEM)] + [hbm] * 4,
        out_specs=(vmem, vmem, vmem),
        scratch_shapes=[pltpu.VMEM(v.shape, v.dtype) for v in operands]
        + [pltpu.SemaphoreType.DMA((4,))],
        compiler_params=pltpu.CompilerParams(vmem_limit_bytes=16 * 1024 * 1024),
    )(expert, *operands)


def shards(tokens, cotangent, expert_slot, gate_fixed, w_gate, w_up, w_down):
    block_x, block_cot = tokens[0], cotangent[0]
    width = block_x.shape[1]
    half = width // 2
    h = w_gate.shape[1]
    own_expert = lax.axis_index("ep") // (NX * NY // E_WIN)
    upper = lax.axis_index("pp") >= lax.axis_size("pp") // 2

    own, other, select = pack(
        own_expert.reshape(1).astype(jnp.int32), expert_slot, gate_fixed, block_x, block_cot
    )
    swapped = swap_x_outer(other)
    mine = jnp.concatenate([w_gate[0], w_up[0], w_down[0]], axis=0)
    theirs = swap_x_pair(mine)
    swapped = after(swapped, mine)
    chunk = jnp.concatenate([own, swapped], axis=0)

    right = left = chunk
    rights, lefts = [], []
    for step in range(4):
        if step == WEIGHT_STEP:
            right = after(right, theirs)
        if step == 3 and HALVES:
            right = shift_y(right[: 2 * CAP], 1)
            left = shift_y(left[2 * CAP :], -1)
            rights.append(jnp.concatenate([right, left], axis=0))
            break
        right = shift_y(right, 1)
        rights.append(right)
        if step < 3:
            left = shift_y(left, -1)
            lefts.append(left)
    near = [chunk] + lefts + rights[::-1]
    parts = [p.reshape(2, 2, CAP, width) for p in near]
    rows_x = jnp.concatenate([p[:, 0].reshape(2 * CAP, width) for p in parts], axis=0)
    rows_c = jnp.concatenate([p[:, 1].reshape(2 * CAP, width) for p in parts], axis=0)

    w_gu = jnp.concatenate([mine[: 2 * h], theirs[: 2 * h]], axis=0)
    w_d = jnp.concatenate([mine[2 * h :], theirs[2 * h :]], axis=0)
    pre = dot(rows_x, w_gu, ((1,), (1,)))
    gate_pre = jnp.concatenate([pre[:, :h], pre[:, 2 * h : 3 * h]], axis=1)
    up_pre = jnp.concatenate([pre[:, h : 2 * h], pre[:, 3 * h :]], axis=1)
    sig = jax.nn.sigmoid(gate_pre)
    activated = gate_pre * sig
    hidden = (activated * up_pre).astype(BF)
    hidden_cot = dot(rows_c, w_d, ((1,), (1,)))
    gate_cot = (hidden_cot * up_pre * (sig * (1.0 + gate_pre * (1.0 - sig)))).astype(BF)
    up_cot = (hidden_cot * activated).astype(BF)
    gu_cot = jnp.concatenate([gate_cot[:, :h], up_cot[:, :h], gate_cot[:, h:], up_cot[:, h:]], axis=1)

    def keep_send(v):
        low, high = v[:, :half], v[:, half:]
        return jnp.where(upper, high, low), jnp.where(upper, low, high)

    grad_d = dot(hidden, rows_c, ((0,), (0,))).astype(BF)
    keep_own_d, send_own_d = keep_send(grad_d[:h])
    keep_their_d, send_their_d = keep_send(grad_d[h:])
    got_send_d = swap_x_pair(send_their_d)
    grad_gu = dot(gu_cot, rows_x, ((0,), (0,))).astype(BF)
    keep_own, send_own = keep_send(grad_gu[: 2 * h])
    keep_their, send_their = keep_send(grad_gu[2 * h :])
    got_send = swap_x_pair(send_their)
    to_mirror_d = plus(send_own_d, got_send_d)
    from_mirror_d = mirror(to_mirror_d)
    to_mirror = plus(send_own, got_send)
    from_mirror = mirror(to_mirror)
    keep_their = jnp.concatenate([keep_their, keep_their_d], axis=0)
    keep_their = after(keep_their, to_mirror)
    got_keep = swap_x_pair(keep_their)

    if RS_MODE == "ring":
        partial = dot(after(gu_cot, send_their), w_gu, ((1,), (0,))).astype(BF)
        part = [partial[2 * CAP * i : 2 * CAP * (i + 1)] for i in range(NY)]
        go_right = shift_y(part[4], 1)
        go_left = shift_y(part[5], -1)
        go_right = shift_y(plus(part[3], go_right), 1)
        go_left = shift_y(plus(part[6], go_left), -1)
        go_right = plus(part[2], go_right)
        go_right = after(go_right, to_mirror)
        go_right = shift_y(go_right, 1)
        go_left = shift_y(plus(part[7], go_left), -1)
        go_right = shift_y(plus(part[1], go_right), 1)
        summed = (part[0].astype(F32) + go_right.astype(F32) + go_left.astype(F32)).astype(BF)
    else:
        y = lax.axis_index("ep") % NY
        turned = jnp.concatenate([gu_cot, gu_cot], axis=0)
        turned = lax.dynamic_slice_in_dim(turned, (NY - y) % NY * 2 * CAP, NY * 2 * CAP, 0)
        if X_FIRST:
            turned = after(turned, send_their_d if X_FIRST == 1 else send_their)
        partial = dot(turned, w_gu, ((1,), (0,))).astype(BF)
        groups = [[x * NY + k for k in range(NY)] for x in range(NX)]
        if RS_MODE == "a2a":
            got = lax.all_to_all(partial.reshape(NY, 2 * CAP, width), "ep", 0, 0, axis_index_groups=groups, tiled=True)
            summed = jnp.sum(got.astype(F32), axis=0).astype(BF)
        else:
            summed = lax.psum_scatter(partial, "ep", scatter_dimension=0, axis_index_groups=groups, tiled=True)
    back = swap_x_outer(summed[CAP:])
    branch = dot(select, jnp.concatenate([summed[:CAP], back], axis=0), ((0,), (0,)))
    input_grad = (block_cot.astype(F32) + branch).astype(BF)[None]
    if TIE_END:
        from_mirror = after(from_mirror, input_grad)

    def total(kept, near, far):
        return (kept.astype(F32) + near.astype(F32) + far.astype(F32)).astype(BF)[None]

    return (
        input_grad,
        total(keep_own[:h], got_keep[:h], from_mirror[:h]),
        total(keep_own[h:], got_keep[h : 2 * h], from_mirror[h:]),
        total(keep_own_d, got_keep[2 * h :], from_mirror_d),
    )


WEIGHT_STEP = 9
HALVES = True
RS_MODE = 'a2a'
X_FIRST = 1
TIE_END = False


def solution(mesh):
    wide = P("pp", "ep", None)
    flat = P("pp", "ep")
    return jax.shard_map(
        shards,
        mesh=mesh,
        in_specs=(wide, wide, flat, flat, wide, wide, wide),
        out_specs=(wide, wide, wide, wide),
        check_vma=False,
    )
```

```python
import jax
import jax.numpy as jnp
from jax import lax
from jax.experimental import pallas as pl
from jax.experimental.pallas import tpu as pltpu
from jax.sharding import PartitionSpec as P

E_WIN = 2
CAP = 16
NX = 4
NY = 8
BF = jnp.bfloat16
F32 = jnp.float32


def swap_x_outer(v):
    return lax.ppermute(v, "ep", [(i, (NX - 1 - i // NY) * NY + i % NY) for i in range(NX * NY)])


def swap_x_pair(v):
    return lax.ppermute(v, "ep", [(i, i ^ NY) for i in range(NX * NY)])


def shift_y(v, step):
    return lax.ppermute(
        v, "ep", [(i, i // NY * NY + (i + step) % NY) for i in range(NX * NY)]
    )


def mirror(v):
    n = lax.axis_size("pp")
    return lax.ppermute(v, "pp", [(i, n - 1 - i) for i in range(n)])


def dot(a, b, dims):
    return lax.dot_general(a, b, (dims, ((), ())), preferred_element_type=F32)


def plus(a, b):
    return (a.astype(F32) + b.astype(F32)).astype(BF)


def after(v, *others):
    return lax.optimization_barrier((v, *others))[0]


def pack_kernel(
    expert_ref, slot_hbm, gate_hbm, x_hbm, c_hbm, own_ref, other_ref, select_ref,
    slot_ref, gate_ref, x_ref, c_ref, sems,
):
    pairs = ((slot_hbm, slot_ref), (gate_hbm, gate_ref), (x_hbm, x_ref), (c_hbm, c_ref))
    copies = [pltpu.make_async_copy(src, dst, sems.at[i]) for i, (src, dst) in enumerate(pairs)]
    for copy in copies:
        copy.start()
    copies[0].wait()
    copies[1].wait()
    slots = slot_ref[...]
    n = slots.shape[1]
    expert = expert_ref[0]
    earlier = lax.broadcasted_iota(jnp.int32, (n, n), 0) < lax.broadcasted_iota(jnp.int32, (n, n), 1)
    earlier = jnp.where(earlier, 1.0, 0.0).astype(BF)
    want = lax.broadcasted_iota(jnp.int32, (CAP, n), 0).astype(F32)

    def pick(which):
        named = jnp.where(slots == which, 1.0, 0.0)
        named = jnp.broadcast_to(named, (CAP, n))
        rank = jnp.dot(named.astype(BF), earlier, preferred_element_type=F32)
        return jnp.where(rank == want, named, 0.0)

    mine, theirs = pick(expert), pick(1 - expert)
    first = jnp.where(expert == 0, mine, theirs)
    second = jnp.where(expert == 0, theirs, mine)
    select_ref[...] = jnp.concatenate([first, second], axis=0).astype(BF)
    select = jnp.concatenate([mine, theirs], axis=0)
    gate = jnp.sum(select * (gate_ref[...].astype(F32) / 4096.0), axis=1, keepdims=True)
    select = select.astype(BF)
    copies[2].wait()
    picked = jnp.dot(select, x_ref[...], preferred_element_type=F32).astype(BF)
    own_ref[:CAP] = picked[:CAP]
    other_ref[:CAP] = picked[CAP:]
    copies[3].wait()
    picked = (gate * jnp.dot(select, c_ref[...], preferred_element_type=F32)).astype(BF)
    own_ref[CAP:] = picked[:CAP]
    other_ref[CAP:] = picked[CAP:]


def pack(expert, slots, gates, block_x, block_cot):
    width = block_x.shape[1]
    vmem = pl.BlockSpec(memory_space=pltpu.VMEM)
    hbm = pl.BlockSpec(memory_space=pltpu.HBM)
    operands = (slots, gates, block_x, block_cot)
    return pl.pallas_call(
        pack_kernel,
        out_shape=(
            jax.ShapeDtypeStruct((2 * CAP, width), BF),
            jax.ShapeDtypeStruct((2 * CAP, width), BF),
            jax.ShapeDtypeStruct((E_WIN * CAP, block_x.shape[0]), BF),
        ),
        in_specs=[pl.BlockSpec(memory_space=pltpu.SMEM)] + [hbm] * 4,
        out_specs=(vmem, vmem, vmem),
        scratch_shapes=[pltpu.VMEM(v.shape, v.dtype) for v in operands]
        + [pltpu.SemaphoreType.DMA((4,))],
        compiler_params=pltpu.CompilerParams(vmem_limit_bytes=PACK_VMEM * 1024 * 1024),
    )(expert, *operands)


def expert_kernel(
    place_ref, x_ref, c_ref, mine_ref, theirs_ref,
    partial_ref, first_ref, second_ref, own_ref, their_keep_ref,
):
    h = mine_ref.shape[0] // 3
    rows, width = x_ref.shape
    half = width // 2
    y, expert, upper = place_ref[0], place_ref[1], place_ref[2]

    def both(k):
        return [mine_ref[k * h : (k + 1) * h], theirs_ref[k * h : (k + 1) * h]]

    w_gu = jnp.concatenate(both(0) + both(1), axis=0)
    pre = dot(x_ref[...], w_gu, ((1,), (1,)))
    gate_pre, up_pre = pre[:, : 2 * h], pre[:, 2 * h :]
    sig = 1.0 / (1.0 + jnp.exp(-gate_pre))
    activated = gate_pre * sig
    hidden = (activated * up_pre).astype(BF)
    hidden_cot = dot(c_ref[...], jnp.concatenate(both(2), axis=0), ((1,), (1,)))
    gate_cot = (hidden_cot * up_pre * (sig * (1.0 + gate_pre * (1.0 - sig)))).astype(BF)
    up_cot = (hidden_cot * activated).astype(BF)
    gu_cot = jnp.concatenate([gate_cot, up_cot], axis=1)

    to = lax.broadcasted_iota(jnp.int32, (rows, rows), 0)
    at = lax.broadcasted_iota(jnp.int32, (rows, rows), 1)
    side, block, rank = to // (NY * CAP), to // CAP % NY, to % CAP
    ring = (block - y + NY) % NY
    ring = sum(jnp.where(ring == r, ORDER.index(r), 0) for r in ORDER)
    source = ring * (2 * CAP) + jnp.where(side == expert, 0, CAP) + rank
    move = jnp.where(at == source, 1.0, 0.0).astype(BF)
    moved = dot(move, gu_cot, ((1,), (0,))).astype(BF)
    tile = half // TILES
    for k in range(2 * TILES):
        cols = slice(k * tile, (k + 1) * tile)
        partial_ref[:, cols] = dot(moved, w_gu[:, cols], ((1,), (0,))).astype(BF)

    for k in range(TILES):
        cols = slice(k * tile, (k + 1) * tile)
        for send in (True, False):
            start = (1 - upper if send else upper) * half + k * tile
            start = pl.multiple_of(start, 128)
            down = dot(hidden, c_ref[:, pl.ds(start, tile)], ((0,), (0,))).astype(BF)
            gu = dot(gu_cot, x_ref[:, pl.ds(start, tile)], ((0,), (0,))).astype(BF)
            if send:
                first_ref[:, cols] = down[h:]
                own_ref[2 * h : 3 * h, cols] = down[:h]
                second_ref[:h, cols] = gu[h : 2 * h]
                second_ref[h:, cols] = gu[3 * h :]
                own_ref[:h, cols] = gu[:h]
                own_ref[h : 2 * h, cols] = gu[2 * h : 3 * h]
            else:
                their_keep_ref[:h, cols] = gu[h : 2 * h]
                their_keep_ref[h : 2 * h, cols] = gu[3 * h :]
                their_keep_ref[2 * h :, cols] = down[h:]
                own_ref[3 * h : 4 * h, cols] = gu[:h]
                own_ref[4 * h : 5 * h, cols] = gu[2 * h : 3 * h]
                own_ref[5 * h :, cols] = down[:h]


def experts(place, rows_x, rows_c, mine, theirs):
    rows, width = rows_x.shape
    h, half = mine.shape[0] // 3, width // 2
    vmem = pl.BlockSpec(memory_space=pltpu.VMEM)
    shapes = [(rows, width), (h, half), (2 * h, half), (6 * h, half), (3 * h, half)]
    return pl.pallas_call(
        expert_kernel,
        out_shape=tuple(jax.ShapeDtypeStruct(v, BF) for v in shapes),
        in_specs=[pl.BlockSpec(memory_space=pltpu.SMEM)] + [vmem] * 4,
        out_specs=(vmem,) * len(shapes),
        compiler_params=pltpu.CompilerParams(vmem_limit_bytes=EXPERT_VMEM * 1024 * 1024),
        cost_estimate=pl.CostEstimate(flops=4 * 10**9, bytes_accessed=16 * 2**20, transcendentals=0),
    )(place, rows_x, rows_c, mine, theirs)


def add_kernel(a_ref, b_ref, out_ref):
    out_ref[...] = plus(a_ref[...], b_ref[...])


def add(a, b, at, cost):
    return pl.pallas_call(
        add_kernel,
        grid=(1,),
        out_shape=jax.ShapeDtypeStruct(b.shape, BF),
        in_specs=[pl.BlockSpec(b.shape, lambda i: (at, 0)), pl.BlockSpec(b.shape, lambda i: (0, 0))],
        out_specs=pl.BlockSpec(b.shape, lambda i: (0, 0)),
        compiler_params=pltpu.CompilerParams(vmem_limit_bytes=8 * 1024 * 1024),
        cost_estimate=pl.CostEstimate(flops=cost * 10**9, bytes_accessed=2**20, transcendentals=0),
    )(a, b)


def shards(tokens, cotangent, expert_slot, gate_fixed, w_gate, w_up, w_down):
    block_x, block_cot = tokens[0], cotangent[0]
    width = block_x.shape[1]
    half = width // 2
    h = w_gate.shape[1]
    own_expert = lax.axis_index("ep") // (NX * NY // E_WIN)
    upper = lax.axis_index("pp") >= lax.axis_size("pp") // 2

    own, other, select = pack(
        own_expert.reshape(1).astype(jnp.int32), expert_slot, gate_fixed, block_x, block_cot
    )
    swapped = swap_x_outer(other)
    mine = jnp.concatenate([w_gate[0], w_up[0], w_down[0]], axis=0)
    theirs = swap_x_pair(mine)
    swapped = after(swapped, mine)
    chunk = jnp.concatenate([own, swapped], axis=0)

    right = left = chunk
    rights, lefts = [], []
    for step in range(4):
        if step == WEIGHT_STEP:
            if WEIGHT_SIDE:
                left = after(left, theirs)
            else:
                right = after(right, theirs)
        if step == 3:
            right = shift_y(right[: RIGHT_ROWS * CAP], 1)
            left = shift_y(left[RIGHT_ROWS * CAP :], -1)
            rights.append(jnp.concatenate([right, left], axis=0))
            break
        right = shift_y(right, 1)
        rights.append(right)
        if step < 3:
            left = shift_y(left, -1)
            lefts.append(left)
    near = [chunk] + lefts + rights[::-1]
    near = [near[r] for r in ORDER]
    parts = [p.reshape(2, 2, CAP, width) for p in near]
    rows_x = jnp.concatenate([p[:, 0].reshape(2 * CAP, width) for p in parts], axis=0)
    rows_c = jnp.concatenate([p[:, 1].reshape(2 * CAP, width) for p in parts], axis=0)

    place = jnp.stack([lax.axis_index("ep") % NY, own_expert, upper.astype(jnp.int32)])
    partial, their_send_d, their_send, own, their_keep = experts(
        place.astype(jnp.int32), rows_x, rows_c, mine, theirs
    )

    got_send_d = swap_x_pair(their_send_d)
    got_send = swap_x_pair(their_send)
    from_mirror_d = mirror(add(own, got_send_d, 2, FIRST_COST))
    to_mirror = add(own, got_send, 0, SECOND_COST)
    from_mirror = mirror(to_mirror)
    if X_LAST == 1:
        their_keep = after(their_keep, to_mirror)
    if X_LAST == 2:
        their_keep = after(their_keep, from_mirror_d)
    got_keep = swap_x_pair(their_keep)

    groups = [[x * NY + k for x in pair for k in range(NY)] for pair in ((0, 3), (1, 2))]
    got = lax.all_to_all(
        partial.reshape(2 * NY, CAP, width), "ep", 0, 0, axis_index_groups=groups, tiled=True
    )
    summed = jnp.sum(got.reshape(2, NY, CAP, width).astype(F32), axis=1).astype(BF)
    branch = dot(select, summed.reshape(2 * CAP, width), ((0,), (0,)))
    input_grad = (block_cot.astype(F32) + branch).astype(BF)[None]
    own_keep = own[3 * h :]

    def total(kept, near, far):
        return (kept.astype(F32) + near.astype(F32) + far.astype(F32)).astype(BF)[None]

    return (
        input_grad,
        total(own_keep[:h], got_keep[:h], from_mirror[:h]),
        total(own_keep[h : 2 * h], got_keep[h : 2 * h], from_mirror[h:]),
        total(own_keep[2 * h :], got_keep[2 * h :], from_mirror_d),
    )


WEIGHT_STEP = 3
X_LAST = 1
TILES = 2
RIGHT_ROWS = 2
WEIGHT_SIDE = 0
ORDER = (4, 5, 3, 6, 2, 7, 1, 0)
FIRST_COST = 100
SECOND_COST = 100
EXPERT_VMEM = 16
PACK_VMEM = 60


def solution(mesh):
    wide = P("pp", "ep", None)
    flat = P("pp", "ep")
    return jax.shard_map(
        shards,
        mesh=mesh,
        in_specs=(wide, wide, flat, flat, wide, wide, wide),
        out_specs=(wide, wide, wide, wide),
        check_vma=False,
    )
```

```python
import jax
import jax.numpy as jnp
from jax import lax
from jax.experimental import pallas as pl
from jax.experimental.pallas import tpu as pltpu
from jax.sharding import PartitionSpec as P

E_WIN = 2
CAP = 16
NX = 4
NY = 8
BF = jnp.bfloat16
F32 = jnp.float32


def swap_x_outer(v):
    return lax.ppermute(v, "ep", [(i, (NX - 1 - i // NY) * NY + i % NY) for i in range(NX * NY)])


def swap_x_pair(v):
    return lax.ppermute(v, "ep", [(i, i ^ NY) for i in range(NX * NY)])


def shift_y(v, step):
    return lax.ppermute(
        v, "ep", [(i, i // NY * NY + (i + step) % NY) for i in range(NX * NY)]
    )


def mirror(v):
    n = lax.axis_size("pp")
    return lax.ppermute(v, "pp", [(i, n - 1 - i) for i in range(n)])


def dot(a, b, dims):
    return lax.dot_general(a, b, (dims, ((), ())), preferred_element_type=F32)


def plus(a, b):
    return (a.astype(F32) + b.astype(F32)).astype(BF)


def after(v, *others):
    return lax.optimization_barrier((v, *others))[0]


def pack_kernel(
    expert_ref, slot_hbm, gate_hbm, x_hbm, c_hbm, own_ref, other_ref, select_ref,
    slot_ref, gate_ref, x_ref, c_ref, sems,
):
    pairs = ((slot_hbm, slot_ref), (gate_hbm, gate_ref), (x_hbm, x_ref), (c_hbm, c_ref))
    copies = [pltpu.make_async_copy(src, dst, sems.at[i]) for i, (src, dst) in enumerate(pairs)]
    for copy in copies:
        copy.start()
    copies[0].wait()
    copies[1].wait()
    slots = slot_ref[...]
    n = slots.shape[1]
    expert = expert_ref[0]
    earlier = lax.broadcasted_iota(jnp.int32, (n, n), 0) < lax.broadcasted_iota(jnp.int32, (n, n), 1)
    earlier = jnp.where(earlier, 1.0, 0.0).astype(BF)
    want = lax.broadcasted_iota(jnp.int32, (CAP, n), 0).astype(F32)

    def pick(which):
        named = jnp.where(slots == which, 1.0, 0.0)
        named = jnp.broadcast_to(named, (CAP, n))
        rank = jnp.dot(named.astype(BF), earlier, preferred_element_type=F32)
        return jnp.where(rank == want, named, 0.0)

    mine, theirs = pick(expert), pick(1 - expert)
    first = jnp.where(expert == 0, mine, theirs)
    second = jnp.where(expert == 0, theirs, mine)
    select_ref[...] = jnp.concatenate([first] * NY + [second] * NY, axis=0).astype(BF)
    select = jnp.concatenate([mine, theirs], axis=0)
    gate = jnp.sum(select * (gate_ref[...].astype(F32) / 4096.0), axis=1, keepdims=True)
    select = select.astype(BF)
    copies[2].wait()
    picked = jnp.dot(select, x_ref[...], preferred_element_type=F32).astype(BF)
    own_ref[:CAP] = picked[:CAP]
    other_ref[:CAP] = picked[CAP:]
    copies[3].wait()
    picked = (gate * jnp.dot(select, c_ref[...], preferred_element_type=F32)).astype(BF)
    own_ref[CAP:] = picked[:CAP]
    other_ref[CAP:] = picked[CAP:]


def pack(expert, slots, gates, block_x, block_cot):
    width = block_x.shape[1]
    vmem = pl.BlockSpec(memory_space=pltpu.VMEM)
    hbm = pl.BlockSpec(memory_space=pltpu.HBM)
    operands = (slots, gates, block_x, block_cot)
    return pl.pallas_call(
        pack_kernel,
        out_shape=(
            jax.ShapeDtypeStruct((2 * CAP, width), BF),
            jax.ShapeDtypeStruct((2 * CAP, width), BF),
            jax.ShapeDtypeStruct((E_WIN * NY * CAP, block_x.shape[0]), BF),
        ),
        in_specs=[pl.BlockSpec(memory_space=pltpu.SMEM)] + [hbm] * 4,
        out_specs=(vmem, vmem, vmem),
        scratch_shapes=[pltpu.VMEM(v.shape, v.dtype) for v in operands]
        + [pltpu.SemaphoreType.DMA((4,))],
        compiler_params=pltpu.CompilerParams(vmem_limit_bytes=PACK_VMEM * 1024 * 1024),
    )(expert, *operands)


def activations(x, c, w_gu, w_d):
    pre = dot(x, w_gu, ((1,), (1,)))
    units = pre.shape[1] // 2
    gate_pre, up_pre = pre[:, :units], pre[:, units:]
    sig = 1.0 / (1.0 + jnp.exp(-gate_pre))
    activated = gate_pre * sig
    hidden = (activated * up_pre).astype(BF)
    hidden_cot = dot(c, w_d, ((1,), (1,)))
    gate_cot = (hidden_cot * up_pre * (sig * (1.0 + gate_pre * (1.0 - sig)))).astype(BF)
    up_cot = (hidden_cot * activated).astype(BF)
    return hidden, jnp.concatenate([gate_cot, up_cot], axis=1)


def weights(mine_ref, theirs_ref):
    h = mine_ref.shape[0] // 3
    parts = [ref[k * h : (k + 1) * h] for k in range(3) for ref in (mine_ref, theirs_ref)]
    return jnp.concatenate(parts[:4], axis=0), jnp.concatenate(parts[4:], axis=0)


def turn(v):
    return jnp.transpose(v.astype(F32)).astype(BF)


def near_kernel(place_ref, x_ref, c_ref, mine_ref, theirs_ref, partial_ref, send_ref, keep_ref):
    rows, width = x_ref.shape
    half = width // 2
    tile = half // TILES
    y, expert, upper = place_ref[0], place_ref[1], place_ref[2]
    w_gu, w_d = weights(mine_ref, theirs_ref)
    hidden, gu_cot = activations(x_ref[...], c_ref[...], w_gu, w_d)

    shape = (partial_ref.shape[0], rows)
    to = lax.broadcasted_iota(jnp.int32, shape, 0)
    at = lax.broadcasted_iota(jnp.int32, shape, 1)
    side, block, rank = to // (NY * CAP), to // CAP % NY, to % CAP
    ring = (block - y + NY) % NY
    chunk = sum(jnp.where(ring == r, ORDER.index(r), 0) for r in ORDER)
    source = chunk * (2 * CAP) + jnp.where(side == expert, 0, CAP) + rank
    move = jnp.where((at == source) & (ring != FAR), 1.0, 0.0).astype(BF)
    moved = dot(move, gu_cot, ((1,), (0,))).astype(BF)
    for k in range(2 * TILES):
        cols = slice(k * tile, (k + 1) * tile)
        partial_ref[:, cols] = dot(moved, w_gu[:, cols], ((1,), (0,))).astype(BF)

    hidden_t, gu_t = turn(hidden), turn(gu_cot)
    units = gu_t.shape[0]
    for out_ref, side in ((send_ref, 1 - upper), (keep_ref, upper)):
        for k in range(TILES):
            cols = slice(k * tile, (k + 1) * tile)
            at_cols = pl.ds(pl.multiple_of(side * half + k * tile, 128), tile)
            out_ref[:units, cols] = dot(gu_t, x_ref[:, at_cols], ((1,), (0,))).astype(BF)
            out_ref[units:, cols] = dot(hidden_t, c_ref[:, at_cols], ((1,), (0,))).astype(BF)


def pair(right_ref, left_ref, start, cols):
    return jnp.concatenate([ref[start : start + CAP, cols] for ref in (right_ref, left_ref)], axis=0)


def far_kernel(
    place_ref, right_ref, left_ref, mine_any, theirs_any, send_any, partial_any,
    partial_out, first_ref, second_ref, own_ref, hidden_ref, cot_ref,
    mine_ref, theirs_ref, send_ref, rows_ref, sems,
):
    loads = ((mine_any, mine_ref), (theirs_any, theirs_ref), (send_any, send_ref))
    loads = [pltpu.make_async_copy(src, dst, sems.at[i]) for i, (src, dst) in enumerate(loads)]
    for copy in loads:
        copy.start()
    h = mine_ref.shape[0] // 3
    half = first_ref.shape[1]
    tile = half // TILES
    y, expert, upper = place_ref[0], place_ref[1], place_ref[2]

    loads[0].wait()
    loads[1].wait()
    w_gu, w_d = weights(mine_ref, theirs_ref)
    everything = slice(0, 2 * half)
    rows_x = pair(right_ref, left_ref, 0, everything)
    rows_c = pair(right_ref, left_ref, CAP, everything)
    hidden, gu_cot = activations(rows_x, rows_c, w_gu, w_d)
    hidden_ref[...] = hidden
    cot_ref[...] = gu_cot
    for k in range(2 * TILES):
        cols = slice(k * tile, (k + 1) * tile)
        rows_ref[:, cols] = dot(gu_cot, w_gu[:, cols], ((1,), (0,))).astype(BF)
    block = (y + FAR) % NY
    stores = []
    for i, side in enumerate((expert, 1 - expert)):
        start = pl.multiple_of(side * (NY * CAP) + block * CAP, CAP)
        stores.append(
            pltpu.make_async_copy(
                rows_ref.at[pl.ds(i * CAP, CAP)], partial_out.at[pl.ds(start, CAP)], sems.at[3 + i]
            )
        )
        stores[-1].start()

    hidden_t, gu_t = turn(hidden), turn(gu_cot)
    loads[2].wait()
    for k in range(TILES):
        cols = slice(k * tile, (k + 1) * tile)
        at_cols = pl.ds(pl.multiple_of((1 - upper) * half + k * tile, 128), tile)
        gu = dot(gu_t, pair(right_ref, left_ref, 0, at_cols), ((1,), (0,)))
        gu = (gu + send_ref[: 4 * h, cols].astype(F32)).astype(BF)
        down = dot(hidden_t, pair(right_ref, left_ref, CAP, at_cols), ((1,), (0,)))
        down = (down + send_ref[4 * h :, cols].astype(F32)).astype(BF)
        first_ref[:, cols] = down[h:]
        second_ref[:h, cols] = gu[h : 2 * h]
        second_ref[h:, cols] = gu[3 * h :]
        own_ref[:h, cols] = gu[:h]
        own_ref[h : 2 * h, cols] = gu[2 * h : 3 * h]
        own_ref[2 * h :, cols] = down[:h]
    for copy in stores:
        copy.wait()


def keep_kernel(place_ref, right_any, left_any, hidden_ref, cot_ref, keep_any, own_ref, their_ref, right_ref, left_ref, keep_ref, sems):
    loads = ((right_any, right_ref), (left_any, left_ref), (keep_any, keep_ref))
    loads = [pltpu.make_async_copy(src, dst, sems.at[i]) for i, (src, dst) in enumerate(loads)]
    for copy in loads:
        copy.start()
    h = own_ref.shape[0] // 3
    half = own_ref.shape[1]
    tile = half // TILES
    hidden_t, gu_t = turn(hidden_ref[...]), turn(cot_ref[...])
    for copy in loads:
        copy.wait()
    for k in range(TILES):
        cols = slice(k * tile, (k + 1) * tile)
        at_cols = pl.ds(pl.multiple_of(place_ref[2] * half + k * tile, 128), tile)
        gu = dot(gu_t, pair(right_ref, left_ref, 0, at_cols), ((1,), (0,)))
        gu = (gu + keep_ref[: 4 * h, cols].astype(F32)).astype(BF)
        down = dot(hidden_t, pair(right_ref, left_ref, CAP, at_cols), ((1,), (0,)))
        down = (down + keep_ref[4 * h :, cols].astype(F32)).astype(BF)
        own_ref[:h, cols] = gu[:h]
        own_ref[h : 2 * h, cols] = gu[2 * h : 3 * h]
        own_ref[2 * h :, cols] = down[:h]
        their_ref[:h, cols] = gu[h : 2 * h]
        their_ref[h : 2 * h, cols] = gu[3 * h :]
        their_ref[2 * h :, cols] = down[h:]


def kept(place, far, hidden, cot, keep):
    h, half = keep.shape[0] // 6, keep.shape[1]
    vmem = pl.BlockSpec(memory_space=pltpu.VMEM)
    anywhere = pl.BlockSpec(memory_space=pl.ANY)
    return pl.pallas_call(
        keep_kernel,
        out_shape=(jax.ShapeDtypeStruct((3 * h, half), BF),) * 2,
        in_specs=[pl.BlockSpec(memory_space=pltpu.SMEM), anywhere, anywhere, vmem, vmem, anywhere],
        out_specs=(vmem, vmem),
        scratch_shapes=[pltpu.VMEM(v.shape, BF) for v in (*far, keep)] + [pltpu.SemaphoreType.DMA((3,))],
        compiler_params=pltpu.CompilerParams(vmem_limit_bytes=EXPERT_VMEM * 1024 * 1024),
        cost_estimate=pl.CostEstimate(flops=10**9, bytes_accessed=8 * 2**20, transcendentals=0),
    )(place, *far, hidden, cot, keep)


def experts(place, rows_x, rows_c, far, mine, theirs):
    width = rows_x.shape[1]
    h, half = mine.shape[0] // 3, width // 2
    vmem = pl.BlockSpec(memory_space=pltpu.VMEM)
    smem = pl.BlockSpec(memory_space=pltpu.SMEM)
    anywhere = pl.BlockSpec(memory_space=pl.ANY)
    params = pltpu.CompilerParams(vmem_limit_bytes=EXPERT_VMEM * 1024 * 1024)

    def arrays(*shapes):
        return tuple(jax.ShapeDtypeStruct(v, BF) for v in shapes)

    near = arrays((2 * NY * CAP, width), (6 * h, half), (6 * h, half))
    partial, send, keep = pl.pallas_call(
        near_kernel,
        out_shape=near,
        in_specs=[smem] + [vmem] * 4,
        out_specs=(vmem,) * 3,
        compiler_params=params,
        cost_estimate=pl.CostEstimate(flops=4 * 10**9, bytes_accessed=16 * 2**20, transcendentals=0),
    )(place, rows_x, rows_c, mine, theirs)
    rows = near[0].shape[0] // NY
    outs = pl.pallas_call(
        far_kernel,
        out_shape=near[:1] + arrays((h, half), (2 * h, half), (3 * h, half), (rows, 2 * h), (rows, 4 * h)),
        in_specs=[smem] + [vmem] * 2 + [anywhere] * 4,
        out_specs=(anywhere,) + (vmem,) * 5,
        scratch_shapes=[pltpu.VMEM(v.shape, BF) for v in (mine, theirs, send)]
        + [pltpu.VMEM((rows, width), BF), pltpu.SemaphoreType.DMA((5,))],
        input_output_aliases={6: 0},
        compiler_params=params,
        cost_estimate=pl.CostEstimate(flops=2 * 10**9, bytes_accessed=8 * 2**20, transcendentals=0),
    )(place, *far, mine, theirs, send, partial)
    return (*outs, keep)


def add_kernel(a_ref, b_ref, out_ref):
    out_ref[...] = plus(a_ref[...], b_ref[...])


def add(a, b, at, cost):
    return pl.pallas_call(
        add_kernel,
        grid=(1,),
        out_shape=jax.ShapeDtypeStruct(b.shape, BF),
        in_specs=[pl.BlockSpec(b.shape, lambda i: (at, 0)), pl.BlockSpec(b.shape, lambda i: (0, 0))],
        out_specs=pl.BlockSpec(b.shape, lambda i: (0, 0)),
        compiler_params=pltpu.CompilerParams(vmem_limit_bytes=8 * 1024 * 1024),
        cost_estimate=pl.CostEstimate(flops=cost * 10**9, bytes_accessed=2**20, transcendentals=0),
    )(a, b)


def shards(tokens, cotangent, expert_slot, gate_fixed, w_gate, w_up, w_down):
    block_x, block_cot = tokens[0], cotangent[0]
    width = block_x.shape[1]
    half = width // 2
    h = w_gate.shape[1]
    own_expert = lax.axis_index("ep") // (NX * NY // E_WIN)
    upper = lax.axis_index("pp") >= lax.axis_size("pp") // 2

    own, other, select = pack(
        own_expert.reshape(1).astype(jnp.int32), expert_slot, gate_fixed, block_x, block_cot
    )
    swapped = swap_x_outer(other)
    mine = jnp.concatenate([w_gate[0], w_up[0], w_down[0]], axis=0)
    theirs = swap_x_pair(mine)
    swapped = after(swapped, mine)
    chunk = jnp.concatenate([own, swapped], axis=0)

    right = left = chunk
    rights, lefts = [], []
    for step in range(4):
        if step == WEIGHT_STEP:
            if WEIGHT_SIDE:
                left = after(left, theirs)
            else:
                right = after(right, theirs)
        if step == 3:
            right = shift_y(right[: 2 * CAP], 1)
            left = shift_y(left[2 * CAP :], -1)
            break
        right = shift_y(right, 1)
        rights.append(right)
        left = shift_y(left, -1)
        lefts.append(left)
    near = dict(enumerate([chunk] + lefts))
    near.update({NY - 1 - i: v for i, v in enumerate(rights)})
    parts = [near[r].reshape(2, 2, CAP, width) for r in ORDER]
    rows_x = jnp.concatenate([p[:, 0].reshape(2 * CAP, width) for p in parts], axis=0)
    rows_c = jnp.concatenate([p[:, 1].reshape(2 * CAP, width) for p in parts], axis=0)

    place = jnp.stack([lax.axis_index("ep") % NY, own_expert, upper.astype(jnp.int32)])
    place = place.astype(jnp.int32)
    partial, their_send_d, their_send, own, hidden, cot, keep = experts(
        place, rows_x, rows_c, (right, left), mine, theirs
    )

    got_send_d = swap_x_pair(their_send_d)
    got_send = swap_x_pair(their_send)
    to_mirror_d = add(own, got_send_d, 2, FIRST_COST)
    from_mirror_d = mirror(to_mirror_d)
    to_mirror = add(own, got_send, 0, SECOND_COST)
    from_mirror = mirror(to_mirror)
    if X_LAST == 1:
        keep = after(keep, to_mirror)
    if X_LAST == 2:
        keep = after(keep, to_mirror, to_mirror_d)
    own_keep, their_keep = kept(place, (right, left), hidden, cot, keep)
    got_keep = swap_x_pair(their_keep)

    groups = [[x * NY + k for x in pair for k in range(NY)] for pair in ((0, 3), (1, 2))]
    got = lax.all_to_all(
        partial.reshape(2 * NY, CAP, width), "ep", 0, 0, axis_index_groups=groups, tiled=True
    )
    branch = dot(select, got.reshape(2 * NY * CAP, width), ((0,), (0,)))
    input_grad = (block_cot.astype(F32) + branch).astype(BF)[None]
    def total(kept, near, far):
        return (kept.astype(F32) + near.astype(F32) + far.astype(F32)).astype(BF)[None]

    return (
        input_grad,
        total(own_keep[:h], got_keep[:h], from_mirror[:h]),
        total(own_keep[h : 2 * h], got_keep[h : 2 * h], from_mirror[h:]),
        total(own_keep[2 * h :], got_keep[2 * h :], from_mirror_d),
    )


WEIGHT_STEP = 3
X_LAST = 1
TILES = 2
WEIGHT_SIDE = 0
FAR = NY // 2
ORDER = (5, 3, 6, 2, 7, 1, 0)
FIRST_COST = 100
SECOND_COST = 100
EXPERT_VMEM = 16
PACK_VMEM = 60


def solution(mesh):
    wide = P("pp", "ep", None)
    flat = P("pp", "ep")
    return jax.shard_map(
        shards,
        mesh=mesh,
        in_specs=(wide, wide, flat, flat, wide, wide, wide),
        out_specs=(wide, wide, wide, wide),
        check_vma=False,
    )
```

```python
import jax
import jax.numpy as jnp
from jax import lax
from jax.experimental import pallas as pl
from jax.experimental.pallas import tpu as pltpu
from jax.sharding import PartitionSpec as P

E_WIN = 2
CAP = 16
NX = 4
NY = 8
BF = jnp.bfloat16
F32 = jnp.float32


def swap_x_outer(v):
    return lax.ppermute(v, "ep", [(i, (NX - 1 - i // NY) * NY + i % NY) for i in range(NX * NY)])


def swap_x_pair(v):
    return lax.ppermute(v, "ep", [(i, i ^ NY) for i in range(NX * NY)])


def shift_y(v, step):
    return lax.ppermute(
        v, "ep", [(i, i // NY * NY + (i + step) % NY) for i in range(NX * NY)]
    )


def mirror(v):
    n = lax.axis_size("pp")
    return lax.ppermute(v, "pp", [(i, n - 1 - i) for i in range(n)])


def dot(a, b, dims):
    return lax.dot_general(a, b, (dims, ((), ())), preferred_element_type=F32)


def plus(a, b):
    return (a.astype(F32) + b.astype(F32)).astype(BF)


def after(v, *others):
    return lax.optimization_barrier((v, *others))[0]


def pack_kernel(
    expert_ref, slot_hbm, gate_hbm, x_hbm, c_hbm, own_ref, other_ref, select_ref,
    slot_ref, gate_ref, x_ref, c_ref, sems,
):
    pairs = ((slot_hbm, slot_ref), (gate_hbm, gate_ref), (x_hbm, x_ref), (c_hbm, c_ref))
    copies = [pltpu.make_async_copy(src, dst, sems.at[i]) for i, (src, dst) in enumerate(pairs)]
    for copy in copies:
        copy.start()
    copies[0].wait()
    copies[1].wait()
    slots = slot_ref[...]
    n = slots.shape[1]
    expert = expert_ref[0]
    earlier = lax.broadcasted_iota(jnp.int32, (n, n), 0) < lax.broadcasted_iota(jnp.int32, (n, n), 1)
    earlier = jnp.where(earlier, 1.0, 0.0).astype(BF)
    want = lax.broadcasted_iota(jnp.int32, (CAP, n), 0).astype(F32)

    def pick(which):
        named = jnp.where(slots == which, 1.0, 0.0)
        named = jnp.broadcast_to(named, (CAP, n))
        rank = jnp.dot(named.astype(BF), earlier, preferred_element_type=F32)
        return jnp.where(rank == want, named, 0.0)

    mine, theirs = pick(expert), pick(1 - expert)
    first = jnp.where(expert == 0, mine, theirs)
    second = jnp.where(expert == 0, theirs, mine)
    select_ref[...] = jnp.concatenate([first] * NY + [second] * NY, axis=0).astype(BF)
    select = jnp.concatenate([mine, theirs], axis=0)
    gate = jnp.sum(select * (gate_ref[...].astype(F32) / 4096.0), axis=1, keepdims=True)
    select = select.astype(BF)
    copies[2].wait()
    picked = jnp.dot(select, x_ref[...], preferred_element_type=F32).astype(BF)
    own_ref[:CAP] = picked[:CAP]
    other_ref[:CAP] = picked[CAP:]
    copies[3].wait()
    picked = (gate * jnp.dot(select, c_ref[...], preferred_element_type=F32)).astype(BF)
    own_ref[CAP:] = picked[:CAP]
    other_ref[CAP:] = picked[CAP:]


def pack(expert, slots, gates, block_x, block_cot):
    width = block_x.shape[1]
    vmem = pl.BlockSpec(memory_space=pltpu.VMEM)
    hbm = pl.BlockSpec(memory_space=pltpu.HBM)
    operands = (slots, gates, block_x, block_cot)
    return pl.pallas_call(
        pack_kernel,
        out_shape=(
            jax.ShapeDtypeStruct((2 * CAP, width), BF),
            jax.ShapeDtypeStruct((2 * CAP, width), BF),
            jax.ShapeDtypeStruct((E_WIN * NY * CAP, block_x.shape[0]), BF),
        ),
        in_specs=[pl.BlockSpec(memory_space=pltpu.SMEM)] + [hbm] * 4,
        out_specs=(vmem, vmem, vmem),
        scratch_shapes=[pltpu.VMEM(v.shape, v.dtype) for v in operands]
        + [pltpu.SemaphoreType.DMA((4,))],
        compiler_params=pltpu.CompilerParams(vmem_limit_bytes=PACK_VMEM * 1024 * 1024),
    )(expert, *operands)


def activations(x, c, w_gu, w_d):
    pre = dot(x, w_gu, ((1,), (1,)))
    units = pre.shape[1] // 2
    gate_pre, up_pre = pre[:, :units], pre[:, units:]
    sig = 1.0 / (1.0 + jnp.exp(-gate_pre))
    activated = gate_pre * sig
    hidden = (activated * up_pre).astype(BF)
    hidden_cot = dot(c, w_d, ((1,), (1,)))
    gate_cot = (hidden_cot * up_pre * (sig * (1.0 + gate_pre * (1.0 - sig)))).astype(BF)
    up_cot = (hidden_cot * activated).astype(BF)
    return hidden, jnp.concatenate([gate_cot, up_cot], axis=1)


def weights(mine_ref, theirs_ref):
    h = mine_ref.shape[0] // 3
    parts = [ref[k * h : (k + 1) * h] for k in range(3) for ref in (mine_ref, theirs_ref)]
    return jnp.concatenate(parts[:4], axis=0), jnp.concatenate(parts[4:], axis=0)


def turn(v):
    return jnp.transpose(v.astype(F32)).astype(BF)


def near_kernel(place_ref, x_ref, c_ref, mine_ref, theirs_ref, partial_ref, send_ref, keep_ref):
    rows, width = x_ref.shape
    half = width // 2
    tile = half // TILES
    y, expert, upper = place_ref[0], place_ref[1], place_ref[2]
    w_gu, w_d = weights(mine_ref, theirs_ref)
    hidden, gu_cot = activations(x_ref[...], c_ref[...], w_gu, w_d)

    shape = (partial_ref.shape[0], rows)
    to = lax.broadcasted_iota(jnp.int32, shape, 0)
    at = lax.broadcasted_iota(jnp.int32, shape, 1)
    side, block, rank = to // (NY * CAP), to // CAP % NY, to % CAP
    ring = (block - y + NY) % NY
    chunk = sum(jnp.where(ring == r, ORDER.index(r), 0) for r in ORDER)
    source = chunk * (2 * CAP) + jnp.where(side == expert, 0, CAP) + rank
    move = jnp.where((at == source) & (ring != FAR), 1.0, 0.0).astype(BF)
    moved = dot(move, gu_cot, ((1,), (0,))).astype(BF)
    for k in range(2 * TILES):
        cols = slice(k * tile, (k + 1) * tile)
        partial_ref[:, cols] = dot(moved, w_gu[:, cols], ((1,), (0,))).astype(BF)

    hidden_t, gu_t = turn(hidden), turn(gu_cot)
    units = gu_t.shape[0]
    for out_ref, side in ((send_ref, 1 - upper), (keep_ref, upper)):
        for k in range(TILES):
            cols = slice(k * tile, (k + 1) * tile)
            at_cols = pl.ds(pl.multiple_of(side * half + k * tile, 128), tile)
            out_ref[:units, cols] = dot(gu_t, x_ref[:, at_cols], ((1,), (0,))).astype(BF)
            out_ref[units:, cols] = dot(hidden_t, c_ref[:, at_cols], ((1,), (0,))).astype(BF)


def pair(right_ref, left_ref, start, cols):
    return jnp.concatenate([ref[start : start + CAP, cols] for ref in (right_ref, left_ref)], axis=0)


def far_kernel(
    place_ref, right_ref, left_ref, mine_ref, theirs_ref, send_any, partial_any,
    partial_out, first_ref, second_ref, own_ref,
    send_ref, rows_ref, sems,
):
    load = pltpu.make_async_copy(send_any, send_ref, sems.at[0])
    load.start()
    h = mine_ref.shape[0] // 3
    half = first_ref.shape[1]
    tile = half // TILES
    y, expert, upper = place_ref[0], place_ref[1], place_ref[2]

    w_gu, w_d = weights(mine_ref, theirs_ref)
    everything = slice(0, 2 * half)
    rows_x = pair(right_ref, left_ref, 0, everything)
    rows_c = pair(right_ref, left_ref, CAP, everything)
    hidden, gu_cot = activations(rows_x, rows_c, w_gu, w_d)
    own_ref[3 * h :, : 2 * h] = hidden
    own_ref[3 * h :, 2 * h : 6 * h] = gu_cot
    for k in range(2 * TILES):
        cols = slice(k * tile, (k + 1) * tile)
        rows_ref[:, cols] = dot(gu_cot, w_gu[:, cols], ((1,), (0,))).astype(BF)
    block = (y + FAR) % NY
    stores = []
    for i, side in enumerate((expert, 1 - expert)):
        start = pl.multiple_of(side * (NY * CAP) + block * CAP, CAP)
        stores.append(
            pltpu.make_async_copy(
                rows_ref.at[pl.ds(i * CAP, CAP)], partial_out.at[pl.ds(start, CAP)], sems.at[3 + i]
            )
        )
        stores[-1].start()

    hidden_t, gu_t = turn(hidden), turn(gu_cot)
    load.wait()
    for k in range(TILES):
        cols = slice(k * tile, (k + 1) * tile)
        at_cols = pl.ds(pl.multiple_of((1 - upper) * half + k * tile, 128), tile)
        gu = dot(gu_t, pair(right_ref, left_ref, 0, at_cols), ((1,), (0,)))
        gu = (gu + send_ref[: 4 * h, cols].astype(F32)).astype(BF)
        down = dot(hidden_t, pair(right_ref, left_ref, CAP, at_cols), ((1,), (0,)))
        down = (down + send_ref[4 * h :, cols].astype(F32)).astype(BF)
        first_ref[:, cols] = down[h:]
        second_ref[:h, cols] = gu[h : 2 * h]
        second_ref[h:, cols] = gu[3 * h :]
        own_ref[:h, cols] = gu[:h]
        own_ref[h : 2 * h, cols] = gu[2 * h : 3 * h]
        own_ref[2 * h : 3 * h, cols] = down[:h]
    for copy in stores:
        copy.wait()


def keep_kernel(
    place_ref, right_any, left_any, keep_any, sent_any, own_ref, their_ref, right_ref, left_ref, keep_ref, cot_ref, sems
):
    rows, units = cot_ref.shape
    sent = sent_any.at[pl.ds(units // 2, rows), pl.ds(0, units)]
    loads = ((right_any, right_ref), (left_any, left_ref), (keep_any, keep_ref), (sent, cot_ref))
    loads = [pltpu.make_async_copy(src, dst, sems.at[i]) for i, (src, dst) in enumerate(loads)]
    for copy in loads:
        copy.start()
    h = own_ref.shape[0] // 3
    half = own_ref.shape[1]
    tile = half // TILES
    for copy in loads:
        copy.wait()
    hidden_t, gu_t = turn(cot_ref[:, : 2 * h]), turn(cot_ref[:, 2 * h :])
    for k in range(TILES):
        cols = slice(k * tile, (k + 1) * tile)
        at_cols = pl.ds(pl.multiple_of(place_ref[2] * half + k * tile, 128), tile)
        gu = dot(gu_t, pair(right_ref, left_ref, 0, at_cols), ((1,), (0,)))
        gu = (gu + keep_ref[: 4 * h, cols].astype(F32)).astype(BF)
        down = dot(hidden_t, pair(right_ref, left_ref, CAP, at_cols), ((1,), (0,)))
        down = (down + keep_ref[4 * h :, cols].astype(F32)).astype(BF)
        own_ref[:h, cols] = gu[:h]
        own_ref[h : 2 * h, cols] = gu[2 * h : 3 * h]
        own_ref[2 * h : 3 * h, cols] = down[:h]
        their_ref[:h, cols] = gu[h : 2 * h]
        their_ref[h : 2 * h, cols] = gu[3 * h :]
        their_ref[2 * h :, cols] = down[h:]


def kept(place, far, keep, sent):
    h, half = keep.shape[0] // 6, keep.shape[1]
    vmem = pl.BlockSpec(memory_space=pltpu.VMEM)
    anywhere = pl.BlockSpec(memory_space=pl.ANY)
    return pl.pallas_call(
        keep_kernel,
        out_shape=(jax.ShapeDtypeStruct((3 * h, half), BF),) * 2,
        in_specs=[pl.BlockSpec(memory_space=pltpu.SMEM)] + [anywhere] * 4,
        out_specs=(vmem, vmem),
        scratch_shapes=[pltpu.VMEM(v.shape, BF) for v in (*far, keep)]
        + [pltpu.VMEM((far[0].shape[0], 6 * h), BF), pltpu.SemaphoreType.DMA((4,))],
        compiler_params=pltpu.CompilerParams(vmem_limit_bytes=EXPERT_VMEM * 1024 * 1024),
        cost_estimate=pl.CostEstimate(flops=10**9, bytes_accessed=8 * 2**20, transcendentals=0),
    )(place, *far, keep, sent)


def experts(place, rows_x, rows_c, far, mine, theirs):
    width = rows_x.shape[1]
    h, half = mine.shape[0] // 3, width // 2
    vmem = pl.BlockSpec(memory_space=pltpu.VMEM)
    smem = pl.BlockSpec(memory_space=pltpu.SMEM)
    anywhere = pl.BlockSpec(memory_space=pl.ANY)
    params = pltpu.CompilerParams(vmem_limit_bytes=EXPERT_VMEM * 1024 * 1024)

    def arrays(*shapes):
        return tuple(jax.ShapeDtypeStruct(v, BF) for v in shapes)

    near = arrays((2 * NY * CAP, width), (6 * h, half), (6 * h, half))
    partial, send, keep = pl.pallas_call(
        near_kernel,
        out_shape=near,
        in_specs=[smem] + [vmem] * 4,
        out_specs=(vmem,) * 3,
        compiler_params=params,
        cost_estimate=pl.CostEstimate(flops=4 * 10**9, bytes_accessed=16 * 2**20, transcendentals=0),
    )(place, rows_x, rows_c, mine, theirs)
    rows = near[0].shape[0] // NY
    outs = pl.pallas_call(
        far_kernel,
        out_shape=near[:1] + arrays((h, half), (2 * h, half), (3 * h + rows, half)),
        in_specs=[smem] + [vmem] * 4 + [anywhere] * 2,
        out_specs=(anywhere,) + (vmem,) * 3,
        scratch_shapes=[pltpu.VMEM(send.shape, BF), pltpu.VMEM((rows, width), BF), pltpu.SemaphoreType.DMA((5,))],
        input_output_aliases={6: 0},
        compiler_params=params,
        cost_estimate=pl.CostEstimate(flops=2 * 10**9, bytes_accessed=8 * 2**20, transcendentals=0),
    )(place, *far, mine, theirs, send, partial)
    return (*outs, keep)


def unpack_kernel(got_any, select_ref, cot_ref, out_any, got_ref, out_ref, sems):
    tile = got_ref.shape[1] // UNPACK_STEPS
    blocks = [pl.ds(k * tile, tile) for k in range(UNPACK_STEPS)]
    loads = [
        pltpu.make_async_copy(got_any.at[:, cols], got_ref.at[:, cols], sems.at[0, k])
        for k, cols in enumerate(blocks)
    ]
    stores = [
        pltpu.make_async_copy(out_ref.at[:, cols], out_any.at[:, cols], sems.at[1, k])
        for k, cols in enumerate(blocks)
    ]
    for copy in loads:
        copy.start()
    places = turn(select_ref[...])
    for cols, load, store in zip(blocks, loads, stores):
        load.wait()
        branch = dot(places, got_ref[:, cols], ((1,), (0,)))
        out_ref[:, cols] = (cot_ref[:, cols].astype(F32) + branch).astype(BF)
        store.start()
    for copy in stores:
        copy.wait()


def unpack(got, select, block_cot):
    vmem = pl.BlockSpec(memory_space=pltpu.VMEM)
    anywhere = pl.BlockSpec(memory_space=pl.ANY)
    return pl.pallas_call(
        unpack_kernel,
        out_shape=jax.ShapeDtypeStruct(block_cot.shape, BF),
        in_specs=[anywhere, vmem, vmem],
        out_specs=anywhere,
        scratch_shapes=[
            pltpu.VMEM(got.shape, BF),
            pltpu.VMEM(block_cot.shape, BF),
            pltpu.SemaphoreType.DMA((2, UNPACK_STEPS)),
        ],
        compiler_params=pltpu.CompilerParams(vmem_limit_bytes=16 * 1024 * 1024),
        cost_estimate=pl.CostEstimate(flops=10**9, bytes_accessed=4 * 2**20, transcendentals=0),
    )(got, select, block_cot)


def add_kernel(a_ref, b_ref, out_ref):
    out_ref[...] = plus(a_ref[...], b_ref[...])


def add(a, b, at, cost):
    return pl.pallas_call(
        add_kernel,
        grid=(1,),
        out_shape=jax.ShapeDtypeStruct(b.shape, BF),
        in_specs=[pl.BlockSpec(b.shape, lambda i: (at, 0)), pl.BlockSpec(b.shape, lambda i: (0, 0))],
        out_specs=pl.BlockSpec(b.shape, lambda i: (0, 0)),
        compiler_params=pltpu.CompilerParams(vmem_limit_bytes=8 * 1024 * 1024),
        cost_estimate=pl.CostEstimate(flops=cost * 10**9, bytes_accessed=2**20, transcendentals=0),
    )(a, b)


def shards(tokens, cotangent, expert_slot, gate_fixed, w_gate, w_up, w_down):
    block_x, block_cot = tokens[0], cotangent[0]
    width = block_x.shape[1]
    half = width // 2
    h = w_gate.shape[1]
    own_expert = lax.axis_index("ep") // (NX * NY // E_WIN)
    upper = lax.axis_index("pp") >= lax.axis_size("pp") // 2

    own, other, select = pack(
        own_expert.reshape(1).astype(jnp.int32), expert_slot, gate_fixed, block_x, block_cot
    )
    swapped = swap_x_outer(other)
    mine = jnp.concatenate([w_gate[0], w_up[0], w_down[0]], axis=0)
    theirs = swap_x_pair(mine)
    swapped = after(swapped, mine)
    chunk = jnp.concatenate([own, swapped], axis=0)

    right = left = chunk
    rights, lefts = [], []
    for step in range(4):
        if step == WEIGHT_STEP:
            if WEIGHT_SIDE:
                left = after(left, theirs)
            else:
                right = after(right, theirs)
        if step == 3:
            right = shift_y(right[: 2 * CAP], 1)
            left = shift_y(left[2 * CAP :], -1)
            break
        right = shift_y(right, 1)
        rights.append(right)
        left = shift_y(left, -1)
        lefts.append(left)
    near = dict(enumerate([chunk] + lefts))
    near.update({NY - 1 - i: v for i, v in enumerate(rights)})
    parts = [near[r].reshape(2, 2, CAP, width) for r in ORDER]
    rows_x = jnp.concatenate([p[:, 0].reshape(2 * CAP, width) for p in parts], axis=0)
    rows_c = jnp.concatenate([p[:, 1].reshape(2 * CAP, width) for p in parts], axis=0)

    place = jnp.stack([lax.axis_index("ep") % NY, own_expert, upper.astype(jnp.int32)])
    place = place.astype(jnp.int32)
    partial, their_send_d, their_send, own, keep = experts(
        place, rows_x, rows_c, (right, left), mine, theirs
    )

    got_send_d = swap_x_pair(their_send_d)
    got_send = swap_x_pair(their_send)
    to_mirror_d = add(own, got_send_d, 2, FIRST_COST)
    from_mirror_d = mirror(to_mirror_d)
    to_mirror = add(own, got_send, 0, SECOND_COST)
    from_mirror = mirror(to_mirror)
    if X_LAST == 1:
        keep = after(keep, to_mirror)
    if X_LAST == 2:
        keep = after(keep, to_mirror, to_mirror_d)
    own_keep, their_keep = kept(place, (right, left), keep, own)
    got_keep = swap_x_pair(their_keep)

    groups = [[x * NY + k for x in pair for k in range(NY)] for pair in ((0, 3), (1, 2))]
    got = lax.all_to_all(
        partial.reshape(2 * NY, CAP, width), "ep", 0, 0, axis_index_groups=groups, tiled=True
    )
    input_grad = unpack(got.reshape(2 * NY * CAP, width), select, block_cot)[None]

    def total(kept, near, far):
        return (kept.astype(F32) + near.astype(F32) + far.astype(F32)).astype(BF)[None]

    return (
        input_grad,
        total(own_keep[:h], got_keep[:h], from_mirror[:h]),
        total(own_keep[h : 2 * h], got_keep[h : 2 * h], from_mirror[h:]),
        total(own_keep[2 * h :], got_keep[2 * h :], from_mirror_d),
    )


WEIGHT_STEP = 3
X_LAST = 1
TILES = 2
WEIGHT_SIDE = 0
FAR = NY // 2
ORDER = (5, 3, 6, 2, 7, 1, 0)
UNPACK_STEPS = 4
FIRST_COST = 100
SECOND_COST = 100
EXPERT_VMEM = 16
PACK_VMEM = 60


def solution(mesh):
    wide = P("pp", "ep", None)
    flat = P("pp", "ep")
    return jax.shard_map(
        shards,
        mesh=mesh,
        in_specs=(wide, wide, flat, flat, wide, wide, wide),
        out_specs=(wide, wide, wide, wide),
        check_vma=False,
    )
```

```python
import jax
import jax.numpy as jnp
from jax import lax
from jax.experimental import pallas as pl
from jax.experimental.pallas import tpu as pltpu
from jax.sharding import PartitionSpec as P

E_WIN = 2
CAP = 16
NX = 4
NY = 8
BF = jnp.bfloat16
F32 = jnp.float32


def swap_x_outer(v):
    return lax.ppermute(v, "ep", [(i, (NX - 1 - i // NY) * NY + i % NY) for i in range(NX * NY)])


def swap_x_pair(v):
    return lax.ppermute(v, "ep", [(i, i ^ NY) for i in range(NX * NY)])


def shift_y(v, step):
    return lax.ppermute(
        v, "ep", [(i, i // NY * NY + (i + step) % NY) for i in range(NX * NY)]
    )


def mirror(v):
    n = lax.axis_size("pp")
    return lax.ppermute(v, "pp", [(i, n - 1 - i) for i in range(n)])


def dot(a, b, dims):
    return lax.dot_general(a, b, (dims, ((), ())), preferred_element_type=F32)


def plus(a, b):
    return (a.astype(F32) + b.astype(F32)).astype(BF)


def after(v, *others):
    return lax.optimization_barrier((v, *others))[0]


def pack_kernel(
    expert_ref, slot_hbm, gate_hbm, x_hbm, c_hbm, own_ref, other_ref, select_ref,
    slot_ref, gate_ref, x_ref, c_ref, sems,
):
    pairs = ((slot_hbm, slot_ref), (gate_hbm, gate_ref), (x_hbm, x_ref), (c_hbm, c_ref))
    copies = [pltpu.make_async_copy(src, dst, sems.at[i]) for i, (src, dst) in enumerate(pairs)]
    for copy in copies:
        copy.start()
    copies[0].wait()
    copies[1].wait()
    slots = slot_ref[...]
    n = slots.shape[1]
    expert = expert_ref[0]
    earlier = lax.broadcasted_iota(jnp.int32, (n, n), 0) < lax.broadcasted_iota(jnp.int32, (n, n), 1)
    earlier = jnp.where(earlier, 1.0, 0.0).astype(BF)
    want = lax.broadcasted_iota(jnp.int32, (CAP, n), 0).astype(F32)

    def pick(which):
        named = jnp.where(slots == which, 1.0, 0.0)
        named = jnp.broadcast_to(named, (CAP, n))
        rank = jnp.dot(named.astype(BF), earlier, preferred_element_type=F32)
        return jnp.where(rank == want, named, 0.0)

    mine, theirs = pick(expert), pick(1 - expert)
    first = jnp.where(expert == 0, mine, theirs)
    second = jnp.where(expert == 0, theirs, mine)
    select_ref[...] = jnp.concatenate([first] * NY + [second] * NY, axis=0).astype(BF)
    select = jnp.concatenate([mine, theirs], axis=0)
    gate = jnp.sum(select * (gate_ref[...].astype(F32) / 4096.0), axis=1, keepdims=True)
    select = select.astype(BF)
    copies[2].wait()
    picked = jnp.dot(select, x_ref[...], preferred_element_type=F32).astype(BF)
    own_ref[:CAP] = picked[:CAP]
    other_ref[:CAP] = picked[CAP:]
    copies[3].wait()
    picked = (gate * jnp.dot(select, c_ref[...], preferred_element_type=F32)).astype(BF)
    own_ref[CAP:] = picked[:CAP]
    other_ref[CAP:] = picked[CAP:]


def pack(expert, slots, gates, block_x, block_cot):
    width = block_x.shape[1]
    vmem = pl.BlockSpec(memory_space=pltpu.VMEM)
    hbm = pl.BlockSpec(memory_space=pltpu.HBM)
    operands = (slots, gates, block_x, block_cot)
    return pl.pallas_call(
        pack_kernel,
        out_shape=(
            jax.ShapeDtypeStruct((2 * CAP, width), BF),
            jax.ShapeDtypeStruct((2 * CAP, width), BF),
            jax.ShapeDtypeStruct((E_WIN * NY * CAP, block_x.shape[0]), BF),
        ),
        in_specs=[pl.BlockSpec(memory_space=pltpu.SMEM)] + [hbm] * 4,
        out_specs=(vmem, vmem, vmem),
        scratch_shapes=[pltpu.VMEM(v.shape, v.dtype) for v in operands]
        + [pltpu.SemaphoreType.DMA((4,))],
        compiler_params=pltpu.CompilerParams(vmem_limit_bytes=PACK_VMEM * 1024 * 1024),
    )(expert, *operands)


def activations(x, c, w_gu, w_d):
    pre = dot(x, w_gu, ((1,), (1,)))
    units = pre.shape[1] // 2
    gate_pre, up_pre = pre[:, :units], pre[:, units:]
    sig = 1.0 / (1.0 + jnp.exp(-gate_pre))
    activated = gate_pre * sig
    hidden = (activated * up_pre).astype(BF)
    hidden_cot = dot(c, w_d, ((1,), (1,)))
    gate_cot = (hidden_cot * up_pre * (sig * (1.0 + gate_pre * (1.0 - sig)))).astype(BF)
    up_cot = (hidden_cot * activated).astype(BF)
    return hidden, jnp.concatenate([gate_cot, up_cot], axis=1)


def weights(mine_ref, theirs_ref):
    h = mine_ref.shape[0] // 3
    parts = [ref[k * h : (k + 1) * h] for k in range(3) for ref in (mine_ref, theirs_ref)]
    return jnp.concatenate(parts[:4], axis=0), jnp.concatenate(parts[4:], axis=0)


def turn(v):
    return jnp.transpose(v.astype(F32)).astype(BF)


def near_kernel(place_ref, x_ref, c_ref, mine_ref, theirs_ref, partial_ref, send_ref, keep_ref):
    rows, width = x_ref.shape
    half = width // 2
    tile = half // TILES
    y, expert, upper = place_ref[0], place_ref[1], place_ref[2]
    w_gu, w_d = weights(mine_ref, theirs_ref)
    hidden, gu_cot = activations(x_ref[...], c_ref[...], w_gu, w_d)

    shape = (partial_ref.shape[0], rows)
    to = lax.broadcasted_iota(jnp.int32, shape, 0)
    at = lax.broadcasted_iota(jnp.int32, shape, 1)
    side, block, rank = to // (NY * CAP), to // CAP % NY, to % CAP
    ring = (block - y + NY) % NY
    chunk = sum(jnp.where(ring == r, ORDER.index(r), 0) for r in ORDER)
    source = chunk * (2 * CAP) + jnp.where(side == expert, 0, CAP) + rank
    move = jnp.where((at == source) & (ring != FAR), 1.0, 0.0).astype(BF)
    moved = dot(move, gu_cot, ((1,), (0,))).astype(BF)
    for k in range(2 * TILES):
        cols = slice(k * tile, (k + 1) * tile)
        partial_ref[:, cols] = dot(moved, w_gu[:, cols], ((1,), (0,))).astype(BF)

    hidden_t, gu_t = turn(hidden), turn(gu_cot)
    units = gu_t.shape[0]
    for out_ref, side in ((send_ref, 1 - upper), (keep_ref, upper)):
        for k in range(TILES):
            cols = slice(k * tile, (k + 1) * tile)
            at_cols = pl.ds(pl.multiple_of(side * half + k * tile, 128), tile)
            out_ref[:units, cols] = dot(gu_t, x_ref[:, at_cols], ((1,), (0,))).astype(BF)
            out_ref[units:, cols] = dot(hidden_t, c_ref[:, at_cols], ((1,), (0,))).astype(BF)


def pair(right_ref, left_ref, start, cols):
    return jnp.concatenate([ref[start : start + CAP, cols] for ref in (right_ref, left_ref)], axis=0)


def far_kernel(
    place_ref, right_ref, left_ref, mine_ref, theirs_ref, send_any, partial_any,
    partial_out, first_ref, second_ref, own_ref,
    send_ref, rows_ref, sems,
):
    load = pltpu.make_async_copy(send_any, send_ref, sems.at[0])
    load.start()
    h = mine_ref.shape[0] // 3
    half = first_ref.shape[1]
    tile = half // TILES
    y, expert, upper = place_ref[0], place_ref[1], place_ref[2]

    w_gu, w_d = weights(mine_ref, theirs_ref)
    everything = slice(0, 2 * half)
    rows_x = pair(right_ref, left_ref, 0, everything)
    rows_c = pair(right_ref, left_ref, CAP, everything)
    hidden, gu_cot = activations(rows_x, rows_c, w_gu, w_d)
    own_ref[3 * h :, : 2 * h] = hidden
    own_ref[3 * h :, 2 * h : 6 * h] = gu_cot
    for k in range(2 * TILES):
        cols = slice(k * tile, (k + 1) * tile)
        rows_ref[:, cols] = dot(gu_cot, w_gu[:, cols], ((1,), (0,))).astype(BF)
    block = (y + FAR) % NY
    stores = []
    for i, side in enumerate((expert, 1 - expert)):
        start = pl.multiple_of(side * (NY * CAP) + block * CAP, CAP)
        stores.append(
            pltpu.make_async_copy(
                rows_ref.at[pl.ds(i * CAP, CAP)], partial_out.at[pl.ds(start, CAP)], sems.at[3 + i]
            )
        )
        stores[-1].start()

    hidden_t, gu_t = turn(hidden), turn(gu_cot)
    load.wait()
    for k in range(TILES):
        cols = slice(k * tile, (k + 1) * tile)
        at_cols = pl.ds(pl.multiple_of((1 - upper) * half + k * tile, 128), tile)
        gu = dot(gu_t, pair(right_ref, left_ref, 0, at_cols), ((1,), (0,)))
        gu = (gu + send_ref[: 4 * h, cols].astype(F32)).astype(BF)
        down = dot(hidden_t, pair(right_ref, left_ref, CAP, at_cols), ((1,), (0,)))
        down = (down + send_ref[4 * h :, cols].astype(F32)).astype(BF)
        second_ref[:h, cols] = gu[h : 2 * h]
        second_ref[h:, cols] = gu[3 * h : 3 * h + h // 2]
        first_ref[: h // 2, cols] = gu[3 * h + h // 2 :]
        first_ref[h // 2 :, cols] = down[h:]
        own_ref[:h, cols] = gu[:h]
        own_ref[h : 2 * h, cols] = gu[2 * h : 3 * h]
        own_ref[2 * h : 3 * h, cols] = down[:h]
    for copy in stores:
        copy.wait()


def keep_kernel(
    place_ref, right_any, left_any, keep_any, sent_any, own_ref, their_ref, right_ref, left_ref, keep_ref, cot_ref, sems
):
    rows, units = cot_ref.shape
    sent = sent_any.at[pl.ds(units // 2, rows), pl.ds(0, units)]
    loads = ((right_any, right_ref), (left_any, left_ref), (keep_any, keep_ref), (sent, cot_ref))
    loads = [pltpu.make_async_copy(src, dst, sems.at[i]) for i, (src, dst) in enumerate(loads)]
    for copy in loads:
        copy.start()
    h = own_ref.shape[0] // 3
    half = own_ref.shape[1]
    tile = half // TILES
    for copy in loads:
        copy.wait()
    hidden_t, gu_t = turn(cot_ref[:, : 2 * h]), turn(cot_ref[:, 2 * h :])
    for k in range(TILES):
        cols = slice(k * tile, (k + 1) * tile)
        at_cols = pl.ds(pl.multiple_of(place_ref[2] * half + k * tile, 128), tile)
        gu = dot(gu_t, pair(right_ref, left_ref, 0, at_cols), ((1,), (0,)))
        gu = (gu + keep_ref[: 4 * h, cols].astype(F32)).astype(BF)
        down = dot(hidden_t, pair(right_ref, left_ref, CAP, at_cols), ((1,), (0,)))
        down = (down + keep_ref[4 * h :, cols].astype(F32)).astype(BF)
        own_ref[:h, cols] = gu[:h]
        own_ref[h : 2 * h, cols] = gu[2 * h : 3 * h]
        own_ref[2 * h : 3 * h, cols] = down[:h]
        their_ref[:h, cols] = gu[h : 2 * h]
        their_ref[h : 2 * h, cols] = gu[3 * h :]
        their_ref[2 * h :, cols] = down[h:]


def kept(place, far, keep, sent):
    h, half = keep.shape[0] // 6, keep.shape[1]
    vmem = pl.BlockSpec(memory_space=pltpu.VMEM)
    anywhere = pl.BlockSpec(memory_space=pl.ANY)
    return pl.pallas_call(
        keep_kernel,
        out_shape=(jax.ShapeDtypeStruct((3 * h, half), BF),) * 2,
        in_specs=[pl.BlockSpec(memory_space=pltpu.SMEM)] + [anywhere] * 4,
        out_specs=(vmem, vmem),
        scratch_shapes=[pltpu.VMEM(v.shape, BF) for v in (*far, keep)]
        + [pltpu.VMEM((far[0].shape[0], 6 * h), BF), pltpu.SemaphoreType.DMA((4,))],
        compiler_params=pltpu.CompilerParams(vmem_limit_bytes=EXPERT_VMEM * 1024 * 1024),
        cost_estimate=pl.CostEstimate(flops=10**9, bytes_accessed=8 * 2**20, transcendentals=0),
    )(place, *far, keep, sent)


def experts(place, rows_x, rows_c, far, mine, theirs):
    width = rows_x.shape[1]
    h, half = mine.shape[0] // 3, width // 2
    vmem = pl.BlockSpec(memory_space=pltpu.VMEM)
    smem = pl.BlockSpec(memory_space=pltpu.SMEM)
    anywhere = pl.BlockSpec(memory_space=pl.ANY)
    params = pltpu.CompilerParams(vmem_limit_bytes=EXPERT_VMEM * 1024 * 1024)

    def arrays(*shapes):
        return tuple(jax.ShapeDtypeStruct(v, BF) for v in shapes)

    near = arrays((2 * NY * CAP, width), (6 * h, half), (6 * h, half))
    partial, send, keep = pl.pallas_call(
        near_kernel,
        out_shape=near,
        in_specs=[smem] + [vmem] * 4,
        out_specs=(vmem,) * 3,
        compiler_params=params,
        cost_estimate=pl.CostEstimate(flops=4 * 10**9, bytes_accessed=16 * 2**20, transcendentals=0),
    )(place, rows_x, rows_c, mine, theirs)
    rows = near[0].shape[0] // NY
    outs = pl.pallas_call(
        far_kernel,
        out_shape=near[:1] + arrays((3 * h // 2, half), (3 * h // 2, half), (3 * h + rows, half)),
        in_specs=[smem] + [vmem] * 4 + [anywhere] * 2,
        out_specs=(anywhere,) + (vmem,) * 3,
        scratch_shapes=[pltpu.VMEM(send.shape, BF), pltpu.VMEM((rows, width), BF), pltpu.SemaphoreType.DMA((5,))],
        input_output_aliases={6: 0},
        compiler_params=params,
        cost_estimate=pl.CostEstimate(flops=2 * 10**9, bytes_accessed=8 * 2**20, transcendentals=0),
    )(place, *far, mine, theirs, send, partial)
    return (*outs, keep)


def unpack_kernel(got_any, select_ref, cot_ref, out_any, got_ref, out_ref, sems):
    tile = got_ref.shape[1] // UNPACK_STEPS
    blocks = [pl.ds(k * tile, tile) for k in range(UNPACK_STEPS)]
    loads = [
        pltpu.make_async_copy(got_any.at[:, cols], got_ref.at[:, cols], sems.at[0, k])
        for k, cols in enumerate(blocks)
    ]
    stores = [
        pltpu.make_async_copy(out_ref.at[:, cols], out_any.at[:, cols], sems.at[1, k])
        for k, cols in enumerate(blocks)
    ]
    for copy in loads:
        copy.start()
    places = turn(select_ref[...])
    for cols, load, store in zip(blocks, loads, stores):
        load.wait()
        branch = dot(places, got_ref[:, cols], ((1,), (0,)))
        out_ref[:, cols] = (cot_ref[:, cols].astype(F32) + branch).astype(BF)
        store.start()
    for copy in stores:
        copy.wait()


def unpack(got, select, block_cot):
    vmem = pl.BlockSpec(memory_space=pltpu.VMEM)
    anywhere = pl.BlockSpec(memory_space=pl.ANY)
    return pl.pallas_call(
        unpack_kernel,
        out_shape=jax.ShapeDtypeStruct(block_cot.shape, BF),
        in_specs=[anywhere, vmem, vmem],
        out_specs=anywhere,
        scratch_shapes=[
            pltpu.VMEM(got.shape, BF),
            pltpu.VMEM(block_cot.shape, BF),
            pltpu.SemaphoreType.DMA((2, UNPACK_STEPS)),
        ],
        compiler_params=pltpu.CompilerParams(vmem_limit_bytes=16 * 1024 * 1024),
        cost_estimate=pl.CostEstimate(flops=10**9, bytes_accessed=4 * 2**20, transcendentals=0),
    )(got, select, block_cot)


def add_kernel(a_ref, b_ref, out_ref):
    out_ref[...] = plus(a_ref[...], b_ref[...])


def add(a, b, at, cost):
    return pl.pallas_call(
        add_kernel,
        grid=(1,),
        out_shape=jax.ShapeDtypeStruct(b.shape, BF),
        in_specs=[pl.BlockSpec(b.shape, lambda i: (at, 0)), pl.BlockSpec(b.shape, lambda i: (0, 0))],
        out_specs=pl.BlockSpec(b.shape, lambda i: (0, 0)),
        compiler_params=pltpu.CompilerParams(vmem_limit_bytes=8 * 1024 * 1024),
        cost_estimate=pl.CostEstimate(flops=cost * 10**9, bytes_accessed=2**20, transcendentals=0),
    )(a, b)


def shards(tokens, cotangent, expert_slot, gate_fixed, w_gate, w_up, w_down):
    block_x, block_cot = tokens[0], cotangent[0]
    width = block_x.shape[1]
    half = width // 2
    h = w_gate.shape[1]
    own_expert = lax.axis_index("ep") // (NX * NY // E_WIN)
    upper = lax.axis_index("pp") >= lax.axis_size("pp") // 2

    own, other, select = pack(
        own_expert.reshape(1).astype(jnp.int32), expert_slot, gate_fixed, block_x, block_cot
    )
    swapped = swap_x_outer(other)
    mine = jnp.concatenate([w_gate[0], w_up[0], w_down[0]], axis=0)
    theirs = swap_x_pair(mine)
    swapped = after(swapped, mine)
    chunk = jnp.concatenate([own, swapped], axis=0)

    right = left = chunk
    rights, lefts = [], []
    for step in range(4):
        if step == WEIGHT_STEP:
            if WEIGHT_SIDE:
                left = after(left, theirs)
            else:
                right = after(right, theirs)
        if step == 3:
            right = shift_y(right[: 2 * CAP], 1)
            left = shift_y(left[2 * CAP :], -1)
            break
        right = shift_y(right, 1)
        rights.append(right)
        left = shift_y(left, -1)
        lefts.append(left)
    near = dict(enumerate([chunk] + lefts))
    near.update({NY - 1 - i: v for i, v in enumerate(rights)})
    parts = [near[r].reshape(2, 2, CAP, width) for r in ORDER]
    rows_x = jnp.concatenate([p[:, 0].reshape(2 * CAP, width) for p in parts], axis=0)
    rows_c = jnp.concatenate([p[:, 1].reshape(2 * CAP, width) for p in parts], axis=0)

    place = jnp.stack([lax.axis_index("ep") % NY, own_expert, upper.astype(jnp.int32)])
    place = place.astype(jnp.int32)
    partial, their_send_d, their_send, own, keep = experts(
        place, rows_x, rows_c, (right, left), mine, theirs
    )

    got_send_d = swap_x_pair(their_send_d)
    got_send = swap_x_pair(their_send)
    to_mirror_d = add(own, got_send_d, 1, FIRST_COST)
    from_mirror_d = mirror(to_mirror_d)
    to_mirror = add(own, got_send, 0, SECOND_COST)
    from_mirror = mirror(to_mirror)
    if X_LAST == 1:
        keep = after(keep, to_mirror)
    if X_LAST == 2:
        keep = after(keep, to_mirror, to_mirror_d)
    own_keep, their_keep = kept(place, (right, left), keep, own)
    got_keep = swap_x_pair(their_keep)

    groups = [[x * NY + k for x in pair for k in range(NY)] for pair in ((0, 3), (1, 2))]
    got = lax.all_to_all(
        partial.reshape(2 * NY, CAP, width), "ep", 0, 0, axis_index_groups=groups, tiled=True
    )
    input_grad = unpack(got.reshape(2 * NY * CAP, width), select, block_cot)[None]

    def total(kept, near, far):
        return (kept.astype(F32) + near.astype(F32) + far.astype(F32)).astype(BF)[None]

    far_up = jnp.concatenate([from_mirror[h:], from_mirror_d[: h // 2]], axis=0)
    return (
        input_grad,
        total(own_keep[:h], got_keep[:h], from_mirror[:h]),
        total(own_keep[h : 2 * h], got_keep[h : 2 * h], far_up),
        total(own_keep[2 * h :], got_keep[2 * h :], from_mirror_d[h // 2 :]),
    )


WEIGHT_STEP = 3
X_LAST = 1
TILES = 2
WEIGHT_SIDE = 0
FAR = NY // 2
ORDER = (5, 3, 6, 2, 7, 1, 0)
UNPACK_STEPS = 4
FIRST_COST = 100
SECOND_COST = 100
EXPERT_VMEM = 16
PACK_VMEM = 60


def solution(mesh):
    wide = P("pp", "ep", None)
    flat = P("pp", "ep")
    return jax.shard_map(
        shards,
        mesh=mesh,
        in_specs=(wide, wide, flat, flat, wide, wide, wide),
        out_specs=(wide, wide, wide, wide),
        check_vma=False,
    )
```
